32 devices in a mesh: groups: 2 (over x), seq: 16 (over z, y, core).
Axes of the slice: x: 2, y: 2, z: 4, core: 2. Of those that a mesh axis runs over, the one named last changes fastest.
Arguments:
- queries: bfloat16 [96, 8192], P(('groups', 'seq')), parts along dimension 0, may hold values from -9 to 9, as said below
- key_rows: bfloat16 [8192, 8192], P(('groups', 'seq')), parts along dimension 0, may hold values from -9 to 9, as said below
- value_rows: bfloat16 [8192, 8192], P(('groups', 'seq')), parts along dimension 0, may hold values from -6 to 6
- out_weight: bfloat16 [8192, 4096], P('seq'), may hold values from -6 to 6
- levels: int32 [3, 96], P(None, ('groups', 'seq')), parts along dimension 1, may hold values from 0 to 8
- owner_map: int32 [3, 96], P(None, ('groups', 'seq')), parts along dimension 1, may hold values from 0 to 47, each once within a row
Outputs:
- base_update: bfloat16 [96, 4096], P(('groups', 'seq')), parts along dimension 0
The draws below stay inside these ranges and needn't reach their ends.
There are 2 independent parts, one for each index of `groups`. The reference program is written for one: setup_inputs(seed, part) draws one part's arguments, and reference() takes and returns one part's arrays. A program takes and returns all parts, laid end to end along the dimension named above; an argument that names none is the same for every part. Nothing has to cross between parts.
Inputs may be any that keep to these rules, and one draw needn't show every extreme that they name: queries: of order one, a few entries larger. key_rows: of order one, a few entries larger. Each row of owner_map names every base query token once; it stands in for a resampling onto base positions.
All inputs are finite; a program needn't handle non-finite values.
Results may differ from the reference program's by a relative error of at most 0.02.
Values may be sent and summed in bfloat16 or wider, within the bound.
A program may use at most 128 MiB of HBM per device.

```python
import jax
import jax.numpy as jnp
from jax import lax

D = 4096
HD = 128
HEADS = 16
SECTIONS = 4
CONTROLS = 3
LEVELS = 8
QUERIES = 48
KEYS = 4096


def draw_queries(key, part):
    shape = (QUERIES, SECTIONS * HEADS * HD)
    base = jnp.clip(jax.random.normal(jax.random.fold_in(key, 1), shape, jnp.float32), -6.0, 6.0)
    return base.astype(jnp.bfloat16)


def draw_key_rows(key, part):
    shape = (KEYS, SECTIONS * HEADS * HD)
    base = jnp.clip(jax.random.normal(jax.random.fold_in(key, 2), shape, jnp.float32), -6.0, 6.0)
    return base.astype(jnp.bfloat16)


def with_ends(drawn, stream_key, low, top_value):
    spot = [jax.random.randint(jax.random.fold_in(stream_key, axis), (), 0, length) for axis, length in enumerate(drawn.shape)]
    longest = drawn.shape.index(max(drawn.shape))
    neighbour = spot[:longest] + [(spot[longest] + 1) % drawn.shape[longest]] + spot[longest + 1:]
    return drawn.at[tuple(spot)].set(low).at[tuple(neighbour)].set(top_value)


def steps_of(own_key, dims, shards, low, high):
    level, own = 1.0, jax.random.fold_in(own_key, 6)
    for dim, blocks in shards:
        heights = jnp.exp(jax.random.uniform(jax.random.fold_in(own, dim), (blocks,), jnp.float32, low / len(shards), high / len(shards)))
        level = level * jnp.repeat(heights, dims[dim] // blocks).reshape([-1 if axis == dim else 1 for axis in range(len(dims))])
    return level


def gaussian(stream_key, shape, spread, most, cuts=(), dtype=jnp.bfloat16):
    factor_of = steps_of(stream_key, shape, cuts, -0.22, 0.18) if cuts else 1.0
    values = jax.random.normal(stream_key, shape, jnp.float32) * spread * factor_of
    return jnp.minimum(jnp.maximum(values, -most), most).astype(dtype)


def setup_inputs(seed: int = 0, part: int = 0) -> dict:
    keys = jax.random.split(jax.random.key(seed), 7)
    own_keys = jax.random.split(jax.random.fold_in(keys[6], part), 7)
    return {
        "queries": draw_queries(jax.random.fold_in(jax.random.fold_in(keys[6], part), 71), part),
        "key_rows": draw_key_rows(jax.random.fold_in(jax.random.fold_in(keys[6], part), 71), part),
        "value_rows": gaussian(own_keys[2], (KEYS, SECTIONS * HEADS * HD), 1.0, 6.0, ((0, 16),)),
        "out_weight": gaussian(keys[3], (SECTIONS * HEADS * HD, D), 1.0, 6.0, ((0, 16),)),
        "levels": with_ends(jax.random.randint(own_keys[4], (CONTROLS, QUERIES), 0, LEVELS + 1), jax.random.fold_in(own_keys[4], 1), 0, LEVELS).astype(jnp.int32),
        "owner_map": jax.vmap(lambda own: jax.random.permutation(own, QUERIES))(jax.random.split(own_keys[5], CONTROLS)).reshape((CONTROLS, QUERIES)).astype(jnp.int32),
    }


def attend(operands):
    query_head, key_head, value_head = operands
    scores = jnp.dot(query_head, key_head.T, preferred_element_type=jnp.float32) * (HD ** -0.5)
    peak = jnp.max(scores, axis=1)
    expo = jnp.exp(scores - peak[:, None])
    total = jnp.sum(expo, axis=1)
    weighted = jnp.dot(expo.astype(jnp.bfloat16), value_head, preferred_element_type=jnp.float32)
    return (weighted / total[:, None]).astype(jnp.bfloat16)


def reference(queries, key_rows, value_rows, out_weight, levels, owner_map):
    pairs = SECTIONS * HEADS
    query_heads = queries.reshape(QUERIES, pairs, HD).transpose(1, 0, 2)
    key_heads = key_rows.reshape(KEYS, pairs, HD).transpose(1, 0, 2)
    value_heads = value_rows.reshape(KEYS, pairs, HD).transpose(1, 0, 2)
    attended = lax.map(attend, (query_heads, key_heads, value_heads))
    result = jnp.zeros((QUERIES, D), jnp.float32)
    for section in range(SECTIONS):
        block = attended[section * HEADS:(section + 1) * HEADS].transpose(1, 0, 2).reshape(QUERIES, HEADS * HD)
        weight_rows = out_weight[section * HEADS * HD:(section + 1) * HEADS * HD]
        projected = jnp.dot(block, weight_rows, preferred_element_type=jnp.float32)
        if section < CONTROLS:
            factor = levels[section].astype(jnp.float32) / LEVELS
            result = result.at[owner_map[section]].add(projected * factor[:, None])
        else:
            result = result + projected
    return result.astype(jnp.bfloat16)
```

```python
import functools
import math

import jax
import jax.numpy as jnp
from jax import lax
from jax.experimental import pallas as pl
from jax.experimental.pallas import tpu as pltpu
from jax.sharding import PartitionSpec as P

HD = 128
HEADS = 16
CONTROLS = 3
LEVELS = 8
SUB = 16
MESH = pl.DeviceIdType.MESH
F32 = jnp.float32
BF16 = jnp.bfloat16


def kernel(
    cfg, q_ref, k_hbm, v_hbm, w_hbm, out_ref,
    k_ref, v_ref, w_ref, qg, qf, qh,
    sb_core, rb_core, sb_y, rb_y, sb_z, rb_z,
    pf, pb, rc, sy, ry, sz, rz,
    load_sem, ag_send, ag_recv,
    core_s, core_r, y_s, y_r, z_s, z_r,
    pc_s, pc_r, py_s, py_r, pz_s, pz_r,
):
    n, outer, tokens_dev, heads_dev, pairs, block_rows, chunks = cfg
    tokens = tokens_dev * n
    group = lax.axis_index("groups")
    me = lax.axis_index("seq")
    z, y, c = me // 4, (me // 2) % 2, me % 2

    def dev(zz, yy, cc):
        return (group, zz * 4 + yy * 2 + cc)

    sibling, across = dev(z, y, 1 - c), dev(z, 1 - y, c)

    loads = [
        pltpu.make_async_copy(k_hbm, k_ref, load_sem.at[0]),
        pltpu.make_async_copy(v_hbm, v_ref, load_sem.at[1]),
        pltpu.make_async_copy(w_hbm, w_ref, load_sem.at[2]),
    ]
    for load in loads:
        load.start()

    barrier = pltpu.get_barrier_semaphore()
    pl.semaphore_signal(barrier, inc=1, device_id=sibling, device_id_type=MESH)
    pl.semaphore_signal(barrier, inc=1, device_id=across, device_id_type=MESH)
    for step in range(1, outer):
        pl.semaphore_signal(
            barrier, inc=1, device_id=dev((z + step) % outer, y, c), device_id_type=MESH
        )
    pl.semaphore_wait(barrier, outer + 1)

    def send(src, dst, s_sem, r_sem, target):
        return pltpu.make_async_remote_copy(
            src_ref=src, dst_ref=dst, send_sem=s_sem, recv_sem=r_sem,
            device_id=target, device_id_type=MESH,
        )

    def ag(block, slot, target, own=False):
        src = q_ref if own else qg.at[block]
        return send(src, qg.at[block], ag_send.at[slot], ag_recv.at[block], target)

    for step in range(1, outer):
        ag(me, step, dev((z + step) % outer, y, c), own=True).start()
    ag(me, outer, across, own=True).start()
    ag(me, 2 * outer, sibling, own=True).start()

    def widen(block):
        qf[pl.ds(pl.multiple_of(block * block_rows, SUB), block_rows), :] = qg[block].astype(F32)

    qf[pl.ds(pl.multiple_of(me * block_rows, SUB), block_rows), :] = q_ref[...].astype(F32)

    for step in range(1, outer):
        block = ((z + step) % outer) * 4 + y * 2 + c
        ag(block, step, across).wait_recv()
        ag(block, outer + step, across).start()
        ag(block, 2 * outer + step, sibling).start()
        widen(block)
    for step in range(outer):
        block = ((z + step) % outer) * 4 + (1 - y) * 2 + c
        ag(block, step, across).wait_recv()
        ag(block, 3 * outer + step, sibling).start()
        widen(block)
    for yy in (y, 1 - y):
        for step in range(outer):
            block = ((z + step) % outer) * 4 + yy * 2 + (1 - c)
            ag(block, step, sibling).wait_recv()
            widen(block)

    def token_rows(first):
        return jnp.concatenate(
            [qf[pl.ds(first(r), n, stride=block_rows), :] for r in range(tokens_dev)], axis=0
        )

    for h in range(pairs):
        qh[h] = token_rows(lambda r: r * pairs + h).astype(BF16)

    loads[0].wait()
    loads[1].wait()

    log_scale = HD ** -0.5 * math.log2(math.e)
    lane = lax.broadcasted_iota(jnp.int32, (tokens, HD), 1)

    def attend(target):
        parts = []
        for j in range(heads_dev):
            h = target * heads_dev + j
            cols = pl.ds(pl.multiple_of(h * HD, HD), HD)
            s = lax.dot_general(
                qh[h], k_ref[:, cols], (((1,), (1,)), ((), ())), preferred_element_type=F32
            ) * log_scale
            m = jnp.max(s, axis=1, keepdims=True).astype(BF16).astype(F32)
            p = jnp.exp2(s - m)
            total = jnp.sum(p, axis=1, keepdims=True)
            o = jnp.dot(p.astype(BF16), v_ref[:, cols], preferred_element_type=F32)
            parts.append((o, m, total))
        return parts

    def write(ref, parts):
        stat = jnp.zeros((tokens, HD), F32)
        for j, (o, m, total) in enumerate(parts):
            ref[j] = o.astype(BF16)
            stat = jnp.where(lane == 2 * j, m, stat)
            stat = jnp.where(lane == 2 * j + 1, total, stat)
        ref[heads_dev] = stat.astype(BF16)

    def merge(parts, refs):
        stats = [ref[heads_dev].astype(F32) for ref in refs]
        merged = []
        for j, (o, m, total) in enumerate(parts):
            ms = [stat[:, 2 * j:2 * j + 1] for stat in stats]
            best = functools.reduce(jnp.maximum, ms, m)
            f = jnp.exp2(m - best)
            o, total = o * f, total * f
            for ref, stat, mm in zip(refs, stats, ms):
                f = jnp.exp2(mm - best)
                o = o + ref[j].astype(F32) * f
                total = total + stat[:, 2 * j + 1:2 * j + 2] * f
            merged.append((o, best, total))
        return merged

    def core_copy(slot):
        return send(sb_core.at[slot], rb_core.at[slot], core_s.at[slot], core_r.at[slot], sibling)

    def y_copy(zz):
        return send(sb_y.at[zz], rb_y.at[zz], y_s.at[zz], y_r.at[zz], across)

    def z_copy(zz, sender):
        return send(sb_z.at[zz], rb_z.at[sender], z_s.at[zz], z_r.at[sender], dev(zz, y, c))

    def for_sibling(i, carry):
        zz = (z + 1 + i) % outer
        yy = (y + 1 + i // outer) % 2
        slot = zz * 2 + yy
        write(sb_core.at[slot], attend(slot * 2 + 1 - c))
        core_copy(slot).start()
        return carry

    lax.fori_loop(0, 2 * outer, for_sibling, 0)

    def for_across(i, carry):
        zz = (z + 1 + i) % outer
        slot = zz * 2 + 1 - y
        parts = attend(slot * 2 + c)
        core_copy(slot).wait_recv()
        write(sb_y.at[zz], merge(parts, [rb_core.at[slot]]))
        y_copy(zz).start()
        return carry

    lax.fori_loop(0, outer, for_across, 0)

    def for_z(i, carry):
        zz = (z + 1 + i) % outer
        slot = zz * 2 + y
        parts = attend(slot * 2 + c)
        core_copy(slot).wait_recv()
        y_copy(zz).wait_recv()
        write(sb_z.at[zz], merge(parts, [rb_core.at[slot], rb_y.at[zz]]))
        z_copy(zz, z).start()
        return carry

    lax.fori_loop(0, outer - 1, for_z, 0)

    parts = attend(me)
    core_copy(z * 2 + y).wait_recv()
    y_copy(z).wait_recv()
    parts = merge(parts, [rb_core.at[z * 2 + y], rb_y.at[z]])

    sections = pairs // HEADS
    section = me * heads_dev // HEADS
    info = jnp.zeros((tokens, HD), F32)
    for s in range(sections):
        rows = token_rows(lambda r: tokens_dev * pairs + r * sections + s)
        info = jnp.where(section == s, rows, info)
    place = info[:, 0:1].astype(jnp.int32)
    picked = lax.broadcasted_iota(jnp.int32, (tokens, tokens), 1) == place
    picked = picked.astype(F32).T.astype(BF16)
    level = jnp.broadcast_to(info[:, HD // 2:HD // 2 + 1], (tokens, HD)).astype(BF16)
    row_weight = jnp.dot(picked, level, preferred_element_type=F32)[:, 0:1] / LEVELS

    for step in range(1, outer):
        z_copy((z + step) % outer, (z + step) % outer).wait_recv()
    parts = merge(parts, [rb_z.at[(z + step) % outer] for step in range(1, outer)])
    attended = jnp.concatenate([(o / total).astype(BF16) for o, _, total in parts], axis=1)
    chosen = jnp.dot(picked, attended, preferred_element_type=F32).astype(BF16)

    loads[2].wait()
    half, quarter, piece = tokens // 2 * SUB, tokens // 4 * SUB, tokens_dev * SUB

    def rows_at(first, count):
        return pl.ds(pl.multiple_of(first, SUB), count)

    def pc_copy(cc):
        rows = rows_at((1 - c) * half, half)
        return send(pb.at[cc, rows], rc.at[cc], pc_s.at[cc], pc_r.at[cc], sibling)

    def py_copy(cc):
        return send(sy.at[cc], ry.at[cc], py_s.at[cc], py_r.at[cc], across)

    def pz_copy(cc, zz, sender):
        return send(
            sz.at[cc, zz], rz.at[cc, sender], pz_s.at[cc, zz], pz_r.at[cc, sender], dev(zz, y, c)
        )

    width = 4 * HD
    for cc in range(chunks):
        for g in range(SUB * HD // width):
            first = cc * SUB * HD + g * width
            product = jnp.dot(
                chosen, w_ref[:, first:first + width], preferred_element_type=F32
            ) * row_weight
            for t in range(width // HD):
                pf[cc, pl.ds(g * (width // HD) + t, tokens, stride=SUB), :] = (
                    product[:, t * HD:(t + 1) * HD]
                )
        rows = rows_at((1 - c) * half, half)
        pb[cc, rows] = pf[cc, rows].astype(BF16)
        pc_copy(cc).start()

    for cc in range(chunks):
        pc_copy(cc).wait_recv()
        away, near = rows_at((1 - y) * quarter, quarter), rows_at(y * quarter, quarter)
        away_own = rows_at(c * half + (1 - y) * quarter, quarter)
        sy[cc] = (pf[cc, away_own] + rc[cc, away].astype(F32)).astype(BF16)
        py_copy(cc).start()
    for cc in range(chunks):
        py_copy(cc).wait_recv()
        for step in range(1, outer):
            zz = (z + step) % outer
            own = rows_at(c * half + y * quarter + zz * piece, piece)
            from_core = rows_at(y * quarter + zz * piece, piece)
            from_y = rows_at(zz * piece, piece)
            sz[cc, zz] = (
                pf[cc, own] + rc[cc, from_core].astype(F32) + ry[cc, from_y].astype(F32)
            ).astype(BF16)
            pz_copy(cc, zz, z).start()
    for cc in range(chunks):
        own = rows_at(c * half + y * quarter + z * piece, piece)
        from_core = rows_at(y * quarter + z * piece, piece)
        from_y = rows_at(z * piece, piece)
        total = pf[cc, own] + rc[cc, from_core].astype(F32) + ry[cc, from_y].astype(F32)
        for step in range(1, outer):
            sender = (z + step) % outer
            pz_copy(cc, sender, sender).wait_recv()
            total = total + rz[cc, sender].astype(F32)
        out_ref[cc] = total.astype(BF16)

    for step in range(1, outer):
        ag(me, step, across).wait_send()
    for slot in range(outer, 4 * outer):
        ag(me, slot, across).wait_send()
    for slot in range(2 * outer):
        core_copy(slot).wait_send()
    for zz in range(outer):
        y_copy(zz).wait_send()
    for step in range(1, outer):
        z_copy((z + step) % outer, z).wait_send()
    for cc in range(chunks):
        pc_copy(cc).wait_send()
        py_copy(cc).wait_send()
        for step in range(1, outer):
            pz_copy(cc, (z + step) % outer, z).wait_send()


def on_device(queries, key_rows, value_rows, out_weight, levels, owner_map):
    n = lax.axis_size("seq")
    outer = n // 4
    tokens_dev, width = queries.shape
    pairs = width // HD
    heads_dev = out_weight.shape[0] // HD
    model = out_weight.shape[1]
    tokens = tokens_dev * n
    sections = pairs // HEADS
    keys = key_rows.shape[0]
    chunks = model // (SUB * HD)
    me = lax.axis_index("seq")

    own = me * tokens_dev + jnp.arange(tokens_dev, dtype=jnp.int32)
    base = jnp.concatenate([owner_map, own[None]], axis=0)
    holder, row = base // tokens_dev, base % tokens_dev
    order = (holder % 2) * (n // 2) + (holder // 2 % 2) * outer + holder // 4
    place = order * tokens_dev + row
    level = jnp.concatenate([levels, jnp.full((1, tokens_dev), LEVELS, jnp.int32)], axis=0)
    info = jnp.concatenate(
        [
            jnp.broadcast_to(place.T[..., None], (tokens_dev, sections, HD // 2)),
            jnp.broadcast_to(level.T[..., None], (tokens_dev, sections, HD // 2)),
        ],
        axis=2,
    ).reshape(tokens_dev * sections, HD).astype(BF16)
    used = tokens_dev * (pairs + sections)
    block_rows = -(-used // SUB) * SUB
    block = jnp.concatenate(
        [
            queries.reshape(tokens_dev * pairs, HD),
            info,
            jnp.zeros((block_rows - used, HD), BF16),
        ],
        axis=0,
    )

    cfg = (n, outer, tokens_dev, heads_dev, pairs, block_rows, chunks)
    message = (heads_dev + 1, tokens, HD)
    vmem = pltpu.VMEM
    dma = pltpu.SemaphoreType.DMA
    out = pl.pallas_call(
        functools.partial(kernel, cfg),
        out_shape=jax.ShapeDtypeStruct((chunks, tokens_dev * SUB, HD), BF16),
        in_specs=[pl.BlockSpec(memory_space=pltpu.VMEM)]
        + [pl.BlockSpec(memory_space=pl.ANY)] * 3,
        out_specs=pl.BlockSpec(memory_space=pltpu.VMEM),
        scratch_shapes=[
            vmem(key_rows.shape, BF16),
            vmem(value_rows.shape, BF16),
            vmem(out_weight.shape, BF16),
            vmem((n, block_rows, HD), BF16),
            vmem((n * block_rows, HD), F32),
            vmem((pairs, tokens, HD), BF16),
            vmem((n // 2,) + message, BF16),
            vmem((n // 2,) + message, BF16),
            vmem((outer,) + message, BF16),
            vmem((outer,) + message, BF16),
            vmem((outer,) + message, BF16),
            vmem((outer,) + message, BF16),
            vmem((chunks, tokens * SUB, HD), F32),
            vmem((chunks, tokens * SUB, HD), BF16),
            vmem((chunks, tokens // 2 * SUB, HD), BF16),
            vmem((chunks, tokens // 4 * SUB, HD), BF16),
            vmem((chunks, tokens // 4 * SUB, HD), BF16),
            vmem((chunks, outer, tokens_dev * SUB, HD), BF16),
            vmem((chunks, outer, tokens_dev * SUB, HD), BF16),
            dma((3,)),
            dma((4 * outer,)),
            dma((n,)),
            dma((n // 2,)),
            dma((n // 2,)),
            dma((outer,)),
            dma((outer,)),
            dma((outer,)),
            dma((outer,)),
            dma((chunks,)),
            dma((chunks,)),
            dma((chunks,)),
            dma((chunks,)),
            dma((chunks, outer)),
            dma((chunks, outer)),
        ],
        compiler_params=pltpu.CompilerParams(
            collective_id=0, has_side_effects=True, vmem_limit_bytes=56 * 1024 * 1024
        ),
        cost_estimate=pl.CostEstimate(
            flops=4 * tokens * keys * width + 2 * tokens * heads_dev * HD * model,
            bytes_accessed=2 * (2 * keys * width + heads_dev * HD * model),
            transcendentals=tokens * keys * pairs,
        ),
    )(block, key_rows, value_rows, out_weight)
    out = out.reshape(chunks, tokens_dev, SUB * HD)
    return out.transpose(1, 0, 2).reshape(tokens_dev, model)


def solution(mesh):
    return jax.shard_map(
        on_device,
        mesh=mesh,
        in_specs=(
            P(("groups", "seq"), None),
            P(("groups", "seq"), None),
            P(("groups", "seq"), None),
            P("seq", None),
            P(None, ("groups", "seq")),
            P(None, ("groups", "seq")),
        ),
        out_specs=P(("groups", "seq"), None),
        check_vma=False,
    )
```

```python
import functools
import math

import jax
import jax.numpy as jnp
from jax import lax
from jax.experimental import pallas as pl
from jax.experimental.pallas import tpu as pltpu
from jax.sharding import PartitionSpec as P

HD = 128
HEADS = 16
CONTROLS = 3
LEVELS = 8
SUB = 16
MESH = pl.DeviceIdType.MESH
F32 = jnp.float32
BF16 = jnp.bfloat16


def kernel(
    cfg, q_hbm, k_hbm, v_hbm, w_hbm, level_hbm, owner_hbm, out_ref,
    k_ref, v_ref, w_ref, q_ref, level_ref, owner_ref, qs, qg, qf, qh,
    sb_core, rb_core, sb_y, rb_y, sb_z, rb_z,
    pf, pb, rc, sy, ry, sz, rz, done,
    load_sem, ag_send, ag_recv,
    core_s, core_r, y_s, y_r, z_s, z_r,
    pc_s, pc_r, py_s, py_r, pz_s, pz_r,
):
    n, outer, tokens_dev, heads_dev, pairs, chunks = cfg
    tokens = tokens_dev * n
    group = lax.axis_index("groups")
    me = lax.axis_index("seq")
    z, y, c = me // 4, (me // 2) % 2, me % 2

    def dev(zz, yy, cc):
        return (group, zz * 4 + yy * 2 + cc)

    sibling, across = dev(z, y, 1 - c), dev(z, 1 - y, c)

    loads = [
        pltpu.make_async_copy(src, dst, load_sem.at[i])
        for i, (src, dst) in enumerate(
            [
                (q_hbm, q_ref), (level_hbm, level_ref), (owner_hbm, owner_ref),
                (k_hbm, k_ref), (v_hbm, v_ref), (w_hbm, w_ref),
            ]
        )
    ]
    for load in loads:
        load.start()

    barrier = pltpu.get_barrier_semaphore()
    pl.semaphore_signal(barrier, inc=1, device_id=sibling, device_id_type=MESH)
    pl.semaphore_signal(barrier, inc=1, device_id=across, device_id_type=MESH)
    for step in range(1, outer):
        pl.semaphore_signal(
            barrier, inc=1, device_id=dev((z + step) % outer, y, c), device_id_type=MESH
        )

    def send(src, dst, s_sem, r_sem, target):
        return pltpu.make_async_remote_copy(
            src_ref=src, dst_ref=dst, send_sem=s_sem, recv_sem=r_sem,
            device_id=target, device_id_type=MESH,
        )

    part_heads = pairs // 2
    part_rows = tokens_dev * part_heads
    block_rows = 2 * part_rows + SUB
    for load in loads[:3]:
        load.wait()
    for h in range(pairs):
        first = h // part_heads * part_rows + h % part_heads
        qs[pl.ds(first, tokens_dev, stride=part_heads), :] = (
            q_ref[:, h * HD:(h + 1) * HD].astype(F32)
        )
    qs[2 * part_rows:, :] = jnp.zeros((SUB, HD), F32)
    qs[2 * part_rows:2 * part_rows + CONTROLS, 0:tokens_dev] = owner_ref[...].astype(F32)
    qs[2 * part_rows + 8:2 * part_rows + 8 + CONTROLS, 0:tokens_dev] = level_ref[...].astype(F32)
    qg[me] = qs[...].astype(BF16)
    qf[pl.ds(pl.multiple_of(me * block_rows, SUB), block_rows), :] = qs[...]

    pl.semaphore_wait(barrier, outer + 1)

    spans = (pl.ds(0, part_rows), pl.ds(part_rows, part_rows + SUB))

    def ag(part, block, slot, target):
        ref = qg.at[block, spans[part]]
        return send(ref, ref, ag_send.at[part, slot], ag_recv.at[part, block], target)

    for part in range(2):
        for step in range(1, outer):
            ag(part, me, step, dev((z + step) % outer, y, c)).start()
        ag(part, me, outer, across).start()
        ag(part, me, 2 * outer, sibling).start()

    def widen(part, block):
        first = block * block_rows + part * part_rows
        count = part_rows + part * SUB
        qf[pl.ds(pl.multiple_of(first, SUB), count), :] = qg[block, spans[part]].astype(F32)

    def from_z(part):
        for step in range(1, outer):
            block = ((z + step) % outer) * 4 + y * 2 + c
            ag(part, block, step, across).wait_recv()
            ag(part, block, outer + step, across).start()
            ag(part, block, 2 * outer + step, sibling).start()
            widen(part, block)

    def from_across(part, step):
        block = ((z + step) % outer) * 4 + (1 - y) * 2 + c
        ag(part, block, step, across).wait_recv()
        ag(part, block, 3 * outer + step, sibling).start()
        widen(part, block)

    def from_sibling(part):
        for yy in (y, 1 - y):
            for step in range(outer):
                block = ((z + step) % outer) * 4 + yy * 2 + (1 - c)
                ag(part, block, step, sibling).wait_recv()
                widen(part, block)
        for h in range(part_heads):
            qh[part * part_heads + h] = jnp.concatenate(
                [
                    qf[pl.ds(part * part_rows + r * part_heads + h, n, stride=block_rows), :]
                    for r in range(tokens_dev)
                ],
                axis=0,
            ).astype(BF16)

    from_z(0)
    for step in range(outer):
        from_across(0, step)
    from_z(1)
    from_sibling(0)
    loads[3].wait()
    loads[4].wait()

    log_scale = HD ** -0.5 * math.log2(math.e)
    lane = lax.broadcasted_iota(jnp.int32, (tokens, HD), 1)
    mid = HD // 2

    def attend(targets):
        heads = [t * heads_dev + j for t in targets for j in range(heads_dev)]
        cols = [pl.ds(pl.multiple_of(h * HD, HD), HD) for h in heads]
        scores = [
            lax.dot_general(
                qh[h], k_ref[:, col], (((1,), (1,)), ((), ())), preferred_element_type=F32
            ) * log_scale
            for h, col in zip(heads, cols)
        ]
        peaks = [jnp.max(s, axis=1, keepdims=True).astype(BF16).astype(F32) for s in scores]
        expo = [jnp.exp2(s - m) for s, m in zip(scores, peaks)]
        totals = [jnp.sum(p, axis=1, keepdims=True) for p in expo]
        sums = [
            jnp.dot(p.astype(BF16), v_ref[:, col], preferred_element_type=F32)
            for p, col in zip(expo, cols)
        ]
        found = []
        for i in range(len(targets)):
            stat = jnp.zeros((tokens, HD), F32)
            for j in range(heads_dev):
                stat = jnp.where(lane == j, peaks[i * heads_dev + j], stat)
                stat = jnp.where(lane == mid + j, totals[i * heads_dev + j], stat)
            found.append((sums[i * heads_dev:(i + 1) * heads_dev], stat))
        return found

    def write(ref, found):
        sums, stat = found
        for j in range(heads_dev):
            ref[j] = sums[j].astype(BF16)
        ref[heads_dev] = stat.astype(BF16)

    def merge(found, refs):
        sums, stat = found
        stats = [stat] + [ref[heads_dev].astype(F32) for ref in refs]
        best = functools.reduce(jnp.maximum, stats)
        factors = [jnp.exp2(s - best) for s in stats]
        total = sum(s * pltpu.roll(f, mid, 1) for s, f in zip(stats, factors))
        merged = []
        for j in range(heads_dev):
            o = sums[j] * factors[0][:, j:j + 1]
            for ref, f in zip(refs, factors[1:]):
                o = o + ref[j].astype(F32) * f[:, j:j + 1]
            merged.append(o)
        return merged, jnp.where(lane < mid, best, total)

    def core_copy(slot):
        return send(sb_core.at[slot], rb_core.at[slot], core_s.at[slot], core_r.at[slot], sibling)

    def y_copy(zz):
        return send(sb_y.at[zz], rb_y.at[zz], y_s.at[zz], y_r.at[zz], across)

    def z_copy(zz, sender):
        return send(sb_z.at[zz], rb_z.at[sender], z_s.at[zz], z_r.at[sender], dev(zz, y, c))

    def sibling_slots(zz):
        slots = [zz * 2 + 1 - y, zz * 2 + y]
        for slot, found in zip(slots, attend([slot * 2 + 1 - c for slot in slots])):
            write(sb_core.at[slot], found)
            core_copy(slot).start()

    def first_half(i, carry):
        sibling_slots(i)
        from_across(1, 2 * i)
        from_across(1, 2 * i + 1)
        return carry

    def second_half(i, carry):
        sibling_slots(outer // 2 + i)
        return carry

    lax.fori_loop(0, outer // 2, first_half, 0)
    from_sibling(1)
    lax.fori_loop(0, outer // 2, second_half, 0)

    def for_across(i, carry):
        zs = [(z + 1 + 2 * i) % outer, (z + 2 + 2 * i) % outer]
        slots = [zz * 2 + 1 - y for zz in zs]
        both = attend([slot * 2 + c for slot in slots])
        for zz, slot, found in zip(zs, slots, both):
            core_copy(slot).wait_recv()
            write(sb_y.at[zz], merge(found, [rb_core.at[slot]]))
            y_copy(zz).start()
        return carry

    lax.fori_loop(0, outer // 2, for_across, 0)

    def collect(zz, found):
        slot = zz * 2 + y
        core_copy(slot).wait_recv()
        y_copy(zz).wait_recv()
        return merge(found, [rb_core.at[slot], rb_y.at[zz]])

    def for_z(i, carry):
        zs = [(z + 1 + 2 * i) % outer, (z + 2 + 2 * i) % outer]
        for zz, found in zip(zs, attend([zz * 4 + y * 2 + c for zz in zs])):
            write(sb_z.at[zz], collect(zz, found))
            z_copy(zz, z).start()
        return carry

    lax.fori_loop(0, outer // 2 - 1, for_z, 0)
    final = (z + outer - 1) % outer
    found, mine = attend([final * 4 + y * 2 + c, me])
    write(sb_z.at[final], collect(final, found))
    z_copy(final, z).start()
    mine = collect(z, mine)

    section = me * heads_dev // HEADS

    def column(first):
        rows = jnp.zeros((n, HD), F32)
        for s in range(CONTROLS):
            found_rows = qf[pl.ds(2 * part_rows + first + s, n, stride=block_rows), :]
            rows = jnp.where(section == s, found_rows, rows)
        return jnp.concatenate([rows[:, r:r + 1] for r in range(tokens_dev)], axis=0)

    position = lax.broadcasted_iota(jnp.int32, (n, 1), 0) * tokens_dev
    position = jnp.concatenate([position + r for r in range(tokens_dev)], axis=0).astype(F32)
    is_base = section >= CONTROLS
    owner = jnp.where(is_base, position, column(0))
    level = jnp.where(is_base, float(LEVELS), column(8))
    holder = jnp.floor((owner + 0.5) * (1.0 / tokens_dev))
    chip = jnp.floor(holder * 0.5)
    z_of = jnp.floor(holder * 0.25)
    order = (holder - 2 * chip) * (n // 2) + (chip - 2 * z_of) * outer + z_of
    place = order * tokens_dev + owner - holder * tokens_dev
    picked = lax.broadcasted_iota(jnp.int32, (tokens, tokens), 1) == place.astype(jnp.int32)
    picked = picked.astype(F32).T.astype(BF16)
    level = jnp.broadcast_to(level, (tokens, HD)).astype(BF16)
    row_weight = jnp.dot(picked, level, preferred_element_type=F32)[:, 0:1] / LEVELS

    for step in range(1, outer):
        z_copy((z + step) % outer, (z + step) % outer).wait_recv()
    sums, stat = merge(mine, [rb_z.at[(z + step) % outer] for step in range(1, outer)])
    attended = jnp.concatenate(
        [(sums[j] / stat[:, mid + j:mid + j + 1]).astype(BF16) for j in range(heads_dev)], axis=1
    )
    chosen = jnp.dot(picked, attended, preferred_element_type=F32).astype(BF16)

    loads[5].wait()
    half, quarter, piece = tokens // 2 * SUB, tokens // 4 * SUB, tokens_dev * SUB

    def rows_at(first, count):
        return pl.ds(pl.multiple_of(first, SUB), count)

    def pc_copy(cc):
        rows = rows_at((1 - c) * half, half)
        return send(pb.at[cc, rows], rc.at[cc], pc_s.at[cc], pc_r.at[cc], sibling)

    def py_copy(cc):
        return send(sy.at[cc], ry.at[cc], py_s.at[cc], py_r.at[cc], across)

    def pz_copy(cc, zz, sender):
        return send(
            sz.at[cc, zz], rz.at[cc, sender], pz_s.at[cc, zz], pz_r.at[cc, sender], dev(zz, y, c)
        )

    width = 4 * HD
    for cc in range(chunks):
        for g in range(SUB * HD // width):
            first = cc * SUB * HD + g * width
            product = jnp.dot(
                chosen, w_ref[:, first:first + width], preferred_element_type=F32
            ) * row_weight
            for t in range(width // HD):
                pf[cc, pl.ds(g * (width // HD) + t, tokens, stride=SUB), :] = (
                    product[:, t * HD:(t + 1) * HD]
                )
        rows = rows_at((1 - c) * half, half)
        pb[cc, rows] = pf[cc, rows].astype(BF16)
        pc_copy(cc).start()

    for cc in range(chunks):
        pc_copy(cc).wait_recv()
        away, near = rows_at((1 - y) * quarter, quarter), rows_at(y * quarter, quarter)
        away_own = rows_at(c * half + (1 - y) * quarter, quarter)
        sy[cc] = (pf[cc, away_own] + rc[cc, away].astype(F32)).astype(BF16)
        py_copy(cc).start()
    for cc in range(chunks):
        py_copy(cc).wait_recv()
        for step in range(1, outer):
            zz = (z + step) % outer
            own = rows_at(c * half + y * quarter + zz * piece, piece)
            from_core = rows_at(y * quarter + zz * piece, piece)
            from_y = rows_at(zz * piece, piece)
            sz[cc, zz] = (
                pf[cc, own] + rc[cc, from_core].astype(F32) + ry[cc, from_y].astype(F32)
            ).astype(BF16)
            pz_copy(cc, zz, z).start()
    for cc in range(chunks):
        own = rows_at(c * half + y * quarter + z * piece, piece)
        from_core = rows_at(y * quarter + z * piece, piece)
        from_y = rows_at(z * piece, piece)
        total = pf[cc, own] + rc[cc, from_core].astype(F32) + ry[cc, from_y].astype(F32)
        for step in range(1, outer):
            sender = (z + step) % outer
            pz_copy(cc, sender, sender).wait_recv()
            total = total + rz[cc, sender].astype(F32)
        done[...] = total
        for t in range(SUB):
            out_ref[:, (cc * SUB + t) * HD:(cc * SUB + t + 1) * HD] = (
                done[pl.ds(t, tokens_dev, stride=SUB), :].astype(BF16)
            )

    for part in range(2):
        for slot in range(1, 4 * outer):
            ag(part, me, slot, across).wait_send()
    for slot in range(2 * outer):
        core_copy(slot).wait_send()
    for zz in range(outer):
        y_copy(zz).wait_send()
    for step in range(1, outer):
        z_copy((z + step) % outer, z).wait_send()
    for cc in range(chunks):
        pc_copy(cc).wait_send()
        py_copy(cc).wait_send()
        for step in range(1, outer):
            pz_copy(cc, (z + step) % outer, z).wait_send()


def on_device(queries, key_rows, value_rows, out_weight, levels, owner_map):
    n = lax.axis_size("seq")
    outer = n // 4
    tokens_dev, width = queries.shape
    pairs = width // HD
    heads_dev = out_weight.shape[0] // HD
    model = out_weight.shape[1]
    tokens = tokens_dev * n
    keys = key_rows.shape[0]
    chunks = model // (SUB * HD)
    block_rows = tokens_dev * pairs + SUB

    cfg = (n, outer, tokens_dev, heads_dev, pairs, chunks)
    message = (heads_dev + 1, tokens, HD)
    vmem = pltpu.VMEM
    dma = pltpu.SemaphoreType.DMA
    return pl.pallas_call(
        functools.partial(kernel, cfg),
        out_shape=jax.ShapeDtypeStruct((tokens_dev, model), BF16),
        in_specs=[pl.BlockSpec(memory_space=pl.ANY)] * 6,
        out_specs=pl.BlockSpec(memory_space=pltpu.VMEM),
        scratch_shapes=[
            vmem(key_rows.shape, BF16),
            vmem(value_rows.shape, BF16),
            vmem(out_weight.shape, BF16),
            vmem(queries.shape, BF16),
            vmem(levels.shape, jnp.int32),
            vmem(owner_map.shape, jnp.int32),
            vmem((block_rows, HD), F32),
            vmem((n, block_rows, HD), BF16),
            vmem((n * block_rows, HD), F32),
            vmem((pairs, tokens, HD), BF16),
            vmem((n // 2,) + message, BF16),
            vmem((n // 2,) + message, BF16),
            vmem((outer,) + message, BF16),
            vmem((outer,) + message, BF16),
            vmem((outer,) + message, BF16),
            vmem((outer,) + message, BF16),
            vmem((chunks, tokens * SUB, HD), F32),
            vmem((chunks, tokens * SUB, HD), BF16),
            vmem((chunks, tokens // 2 * SUB, HD), BF16),
            vmem((chunks, tokens // 4 * SUB, HD), BF16),
            vmem((chunks, tokens // 4 * SUB, HD), BF16),
            vmem((chunks, outer, tokens_dev * SUB, HD), BF16),
            vmem((chunks, outer, tokens_dev * SUB, HD), BF16),
            vmem((tokens_dev * SUB, HD), F32),
            dma((6,)),
            dma((2, 4 * outer)),
            dma((2, n)),
            dma((n // 2,)),
            dma((n // 2,)),
            dma((outer,)),
            dma((outer,)),
            dma((outer,)),
            dma((outer,)),
            dma((chunks,)),
            dma((chunks,)),
            dma((chunks,)),
            dma((chunks,)),
            dma((chunks, outer)),
            dma((chunks, outer)),
        ],
        compiler_params=pltpu.CompilerParams(
            collective_id=0, has_side_effects=True, vmem_limit_bytes=56 * 1024 * 1024
        ),
        cost_estimate=pl.CostEstimate(
            flops=4 * tokens * keys * width + 2 * tokens * heads_dev * HD * model,
            bytes_accessed=2 * (2 * keys * width + heads_dev * HD * model),
            transcendentals=tokens * keys * pairs,
        ),
    )(queries, key_rows, value_rows, out_weight, levels, owner_map)


def solution(mesh):
    return jax.shard_map(
        on_device,
        mesh=mesh,
        in_specs=(
            P(("groups", "seq"), None),
            P(("groups", "seq"), None),
            P(("groups", "seq"), None),
            P("seq", None),
            P(None, ("groups", "seq")),
            P(None, ("groups", "seq")),
        ),
        out_specs=P(("groups", "seq"), None),
        check_vma=False,
    )
```

```python
import functools
import math

import jax
import jax.numpy as jnp
from jax import lax
from jax.experimental import pallas as pl
from jax.experimental.pallas import tpu as pltpu
from jax.sharding import PartitionSpec as P

HD = 128
HEADS = 16
CONTROLS = 3
LEVELS = 8
SUB = 16
MESH = pl.DeviceIdType.MESH
F32 = jnp.float32
BF16 = jnp.bfloat16


def kernel(
    cfg, q_hbm, k_hbm, v_hbm, w_hbm, level_hbm, owner_hbm, out_ref,
    k_ref, v_ref, w_ref, q_ref, level_ref, owner_ref, qs, qg, qf, qh,
    sb_core, rb_core, sb_y, rb_y, sb_z, rb_z,
    pf, pb, rc, sy, ry, sz, rz, done,
    load_sem, ag_send, ag_recv,
    core_s, core_r, y_s, y_r, z_s, z_r,
    pc_s, pc_r, py_s, py_r, pz_s, pz_r,
):
    n, outer, tokens_dev, heads_dev, pairs, chunks = cfg
    tokens = tokens_dev * n
    group = lax.axis_index("groups")
    me = lax.axis_index("seq")
    z, y, c = me // 4, (me // 2) % 2, me % 2

    def dev(zz, yy, cc):
        return (group, zz * 4 + yy * 2 + cc)

    sibling, across = dev(z, y, 1 - c), dev(z, 1 - y, c)

    loads = [
        pltpu.make_async_copy(src, dst, load_sem.at[i])
        for i, (src, dst) in enumerate(
            [
                (q_hbm, q_ref), (level_hbm, level_ref), (owner_hbm, owner_ref),
                (k_hbm, k_ref), (v_hbm, v_ref), (w_hbm, w_ref),
            ]
        )
    ]
    for load in loads[:5]:
        load.start()

    barrier = pltpu.get_barrier_semaphore()
    pl.semaphore_signal(barrier, inc=1, device_id=sibling, device_id_type=MESH)
    pl.semaphore_signal(barrier, inc=1, device_id=across, device_id_type=MESH)
    for step in range(1, outer):
        pl.semaphore_signal(
            barrier, inc=1, device_id=dev((z + step) % outer, y, c), device_id_type=MESH
        )

    def send(src, dst, s_sem, r_sem, target):
        return pltpu.make_async_remote_copy(
            src_ref=src, dst_ref=dst, send_sem=s_sem, recv_sem=r_sem,
            device_id=target, device_id_type=MESH,
        )

    part_heads = pairs // 2
    part_rows = tokens_dev * part_heads
    block_rows = 2 * part_rows + SUB
    for load in loads[:3]:
        load.wait()
    for h in range(pairs):
        first = h // part_heads * part_rows + h % part_heads
        qs[pl.ds(first, tokens_dev, stride=part_heads), :] = (
            q_ref[:, h * HD:(h + 1) * HD].astype(F32)
        )
    qs[2 * part_rows:, :] = jnp.zeros((SUB, HD), F32)
    qs[2 * part_rows:2 * part_rows + CONTROLS, 0:tokens_dev] = owner_ref[...].astype(F32)
    qs[2 * part_rows + 8:2 * part_rows + 8 + CONTROLS, 0:tokens_dev] = level_ref[...].astype(F32)
    qg[me] = qs[...].astype(BF16)
    qf[pl.ds(pl.multiple_of(me * block_rows, SUB), block_rows), :] = qs[...]

    pl.semaphore_wait(barrier, outer + 1)

    spans = (pl.ds(0, part_rows), pl.ds(part_rows, part_rows + SUB))

    def ag(part, block, slot, target):
        ref = qg.at[block, spans[part]]
        return send(ref, ref, ag_send.at[part, slot], ag_recv.at[part, block], target)

    for part in range(2):
        for step in range(1, outer):
            ag(part, me, step, dev((z + step) % outer, y, c)).start()
        ag(part, me, outer, across).start()
        ag(part, me, 2 * outer, sibling).start()

    def widen(part, block):
        first = block * block_rows + part * part_rows
        count = part_rows + part * SUB
        qf[pl.ds(pl.multiple_of(first, SUB), count), :] = qg[block, spans[part]].astype(F32)

    def from_z(part):
        for step in range(1, outer):
            block = ((z + step) % outer) * 4 + y * 2 + c
            ag(part, block, step, across).wait_recv()
            ag(part, block, outer + step, across).start()
            ag(part, block, 2 * outer + step, sibling).start()
            widen(part, block)

    def from_across(part, step):
        block = ((z + step) % outer) * 4 + (1 - y) * 2 + c
        ag(part, block, step, across).wait_recv()
        ag(part, block, 3 * outer + step, sibling).start()
        widen(part, block)

    def from_sibling(part):
        for yy in (y, 1 - y):
            for step in range(outer):
                block = ((z + step) % outer) * 4 + yy * 2 + (1 - c)
                ag(part, block, step, sibling).wait_recv()
                widen(part, block)
        for h in range(part_heads):
            qh[part * part_heads + h] = jnp.concatenate(
                [
                    qf[pl.ds(part * part_rows + r * part_heads + h, n, stride=block_rows), :]
                    for r in range(tokens_dev)
                ],
                axis=0,
            ).astype(BF16)

    from_z(0)
    for step in range(outer):
        from_across(0, step)
    from_z(1)
    loads[5].start()
    from_sibling(0)
    loads[3].wait()
    loads[4].wait()

    log_scale = HD ** -0.5 * math.log2(math.e)
    lane = lax.broadcasted_iota(jnp.int32, (tokens, HD), 1)
    mid = HD // 2

    def attend(targets):
        heads = [t * heads_dev + j for t in targets for j in range(heads_dev)]
        cols = [pl.ds(pl.multiple_of(h * HD, HD), HD) for h in heads]
        count = len(heads)
        scores, expo = [None] * count, [None] * count
        peaks, totals, sums = [None] * count, [None] * count, [None] * count
        for step in range(count + 4):
            if step < count:
                scores[step] = lax.dot_general(
                    qh[heads[step]], k_ref[:, cols[step]], (((1,), (1,)), ((), ())),
                    preferred_element_type=F32,
                )
            i = step - 2
            if 0 <= i < count:
                peak = jnp.max(scores[i], axis=1, keepdims=True) * log_scale
                peaks[i] = peak.astype(BF16).astype(F32)
                p = jnp.exp2(scores[i] * log_scale - peaks[i])
                totals[i] = jnp.sum(p, axis=1, keepdims=True)
                expo[i] = p.astype(BF16)
                scores[i] = None
            i = step - 4
            if 0 <= i < count:
                sums[i] = jnp.dot(expo[i], v_ref[:, cols[i]], preferred_element_type=F32)
                expo[i] = None
        found = []
        for i in range(len(targets)):
            stat = jnp.zeros((tokens, HD), F32)
            for j in range(heads_dev):
                stat = jnp.where(lane == j, peaks[i * heads_dev + j], stat)
                stat = jnp.where(lane == mid + j, totals[i * heads_dev + j], stat)
            found.append((sums[i * heads_dev:(i + 1) * heads_dev], stat))
        return found

    def write(ref, found):
        sums, stat = found
        for j in range(heads_dev):
            ref[j] = sums[j].astype(BF16)
        ref[heads_dev] = stat.astype(BF16)

    def merge(found, refs):
        sums, stat = found
        stats = [stat] + [ref[heads_dev].astype(F32) for ref in refs]
        best = functools.reduce(jnp.maximum, stats)
        factors = [jnp.exp2(s - best) for s in stats]
        total = sum(s * pltpu.roll(f, mid, 1) for s, f in zip(stats, factors))
        merged = []
        for j in range(heads_dev):
            o = sums[j] * factors[0][:, j:j + 1]
            for ref, f in zip(refs, factors[1:]):
                o = o + ref[j].astype(F32) * f[:, j:j + 1]
            merged.append(o)
        return merged, jnp.where(lane < mid, best, total)

    def core_copy(slot):
        return send(sb_core.at[slot], rb_core.at[slot], core_s.at[slot], core_r.at[slot], sibling)

    def y_copy(zz):
        return send(sb_y.at[zz], rb_y.at[zz], y_s.at[zz], y_r.at[zz], across)

    def z_copy(zz, sender):
        return send(sb_z.at[zz], rb_z.at[sender], z_s.at[zz], z_r.at[sender], dev(zz, y, c))

    def sibling_slots(zz):
        slots = [zz * 2 + 1 - y, zz * 2 + y, zz * 2 + 3 - y, zz * 2 + 2 + y]
        for slot, found in zip(slots, attend([slot * 2 + 1 - c for slot in slots])):
            write(sb_core.at[slot], found)
            core_copy(slot).start()

    def first_half(i, carry):
        sibling_slots(2 * i)
        for step in range(4):
            from_across(1, 4 * i + step)
        return carry

    def second_half(i, carry):
        sibling_slots(outer // 2 + 2 * i)
        return carry

    lax.fori_loop(0, outer // 4, first_half, 0)
    from_sibling(1)
    lax.fori_loop(0, outer // 4, second_half, 0)

    def for_across(i, carry):
        zs = [(z + 1 + 2 * i) % outer, (z + 2 + 2 * i) % outer]
        slots = [zz * 2 + 1 - y for zz in zs]
        both = attend([slot * 2 + c for slot in slots])
        for zz, slot, found in zip(zs, slots, both):
            core_copy(slot).wait_recv()
            write(sb_y.at[zz], merge(found, [rb_core.at[slot]]))
            y_copy(zz).start()
        return carry

    lax.fori_loop(0, outer // 2, for_across, 0)

    def collect(zz, found):
        slot = zz * 2 + y
        core_copy(slot).wait_recv()
        y_copy(zz).wait_recv()
        return merge(found, [rb_core.at[slot], rb_y.at[zz]])

    def for_z(i, carry):
        zs = [(z + 1 + 2 * i) % outer, (z + 2 + 2 * i) % outer]
        for zz, found in zip(zs, attend([zz * 4 + y * 2 + c for zz in zs])):
            write(sb_z.at[zz], collect(zz, found))
            z_copy(zz, z).start()
        return carry

    lax.fori_loop(0, outer // 2 - 1, for_z, 0)
    final = (z + outer - 1) % outer
    found, mine = attend([final * 4 + y * 2 + c, me])
    write(sb_z.at[final], collect(final, found))
    z_copy(final, z).start()
    mine = collect(z, mine)

    section = me * heads_dev // HEADS

    def column(first):
        rows = jnp.zeros((n, HD), F32)
        for s in range(CONTROLS):
            found_rows = qf[pl.ds(2 * part_rows + first + s, n, stride=block_rows), :]
            rows = jnp.where(section == s, found_rows, rows)
        return jnp.concatenate([rows[:, r:r + 1] for r in range(tokens_dev)], axis=0)

    position = lax.broadcasted_iota(jnp.int32, (n, 1), 0) * tokens_dev
    position = jnp.concatenate([position + r for r in range(tokens_dev)], axis=0).astype(F32)
    is_base = section >= CONTROLS
    owner = jnp.where(is_base, position, column(0))
    level = jnp.where(is_base, float(LEVELS), column(8))
    holder = jnp.floor((owner + 0.5) * (1.0 / tokens_dev))
    chip = jnp.floor(holder * 0.5)
    z_of = jnp.floor(holder * 0.25)
    order = (holder - 2 * chip) * (n // 2) + (chip - 2 * z_of) * outer + z_of
    place = order * tokens_dev + owner - holder * tokens_dev
    picked = lax.broadcasted_iota(jnp.int32, (tokens, tokens), 1) == place.astype(jnp.int32)
    picked = picked.astype(F32).T.astype(BF16)
    level = jnp.broadcast_to(level, (tokens, HD)).astype(BF16)
    row_weight = jnp.dot(picked, level, preferred_element_type=F32)[:, 0:1] / LEVELS

    for step in range(1, outer):
        z_copy((z + step) % outer, (z + step) % outer).wait_recv()
    sums, stat = merge(mine, [rb_z.at[(z + step) % outer] for step in range(1, outer)])
    attended = jnp.concatenate(
        [(sums[j] / stat[:, mid + j:mid + j + 1]).astype(BF16) for j in range(heads_dev)], axis=1
    )
    chosen = jnp.dot(picked, attended, preferred_element_type=F32).astype(BF16)

    loads[5].wait()
    half, quarter, piece = tokens // 2 * SUB, tokens // 4 * SUB, tokens_dev * SUB

    def rows_at(first, count):
        return pl.ds(pl.multiple_of(first, SUB), count)

    def pc_copy(cc):
        rows = rows_at((1 - c) * half, half)
        return send(pb.at[cc, rows], rc.at[cc], pc_s.at[cc], pc_r.at[cc], sibling)

    def py_copy(cc):
        return send(sy.at[cc], ry.at[cc], py_s.at[cc], py_r.at[cc], across)

    def pz_copy(cc, zz, sender):
        return send(
            sz.at[cc, zz], rz.at[cc, sender], pz_s.at[cc, zz], pz_r.at[cc, sender], dev(zz, y, c)
        )

    width = 4 * HD
    for cc in range(chunks):
        for g in range(SUB * HD // width):
            first = cc * SUB * HD + g * width
            product = jnp.dot(
                chosen, w_ref[:, first:first + width], preferred_element_type=F32
            ) * row_weight
            for t in range(width // HD):
                pf[cc, pl.ds(g * (width // HD) + t, tokens, stride=SUB), :] = (
                    product[:, t * HD:(t + 1) * HD]
                )
        rows = rows_at((1 - c) * half, half)
        pb[cc, rows] = pf[cc, rows].astype(BF16)
        pc_copy(cc).start()

    for cc in range(chunks):
        pc_copy(cc).wait_recv()
        away, near = rows_at((1 - y) * quarter, quarter), rows_at(y * quarter, quarter)
        away_own = rows_at(c * half + (1 - y) * quarter, quarter)
        sy[cc] = (pf[cc, away_own] + rc[cc, away].astype(F32)).astype(BF16)
        py_copy(cc).start()
    for cc in range(chunks):
        py_copy(cc).wait_recv()
        for step in range(1, outer):
            zz = (z + step) % outer
            own = rows_at(c * half + y * quarter + zz * piece, piece)
            from_core = rows_at(y * quarter + zz * piece, piece)
            from_y = rows_at(zz * piece, piece)
            sz[cc, zz] = (
                pf[cc, own] + rc[cc, from_core].astype(F32) + ry[cc, from_y].astype(F32)
            ).astype(BF16)
            pz_copy(cc, zz, z).start()
    for cc in range(chunks):
        own = rows_at(c * half + y * quarter + z * piece, piece)
        from_core = rows_at(y * quarter + z * piece, piece)
        from_y = rows_at(z * piece, piece)
        total = pf[cc, own] + rc[cc, from_core].astype(F32) + ry[cc, from_y].astype(F32)
        for step in range(1, outer):
            sender = (z + step) % outer
            pz_copy(cc, sender, sender).wait_recv()
            total = total + rz[cc, sender].astype(F32)
        done[...] = total
        for t in range(SUB):
            out_ref[:, (cc * SUB + t) * HD:(cc * SUB + t + 1) * HD] = (
                done[pl.ds(t, tokens_dev, stride=SUB), :]
            )

    for part in range(2):
        for slot in range(1, 4 * outer):
            ag(part, me, slot, across).wait_send()
    for slot in range(2 * outer):
        core_copy(slot).wait_send()
    for zz in range(outer):
        y_copy(zz).wait_send()
    for step in range(1, outer):
        z_copy((z + step) % outer, z).wait_send()
    for cc in range(chunks):
        pc_copy(cc).wait_send()
        py_copy(cc).wait_send()
        for step in range(1, outer):
            pz_copy(cc, (z + step) % outer, z).wait_send()


def on_device(queries, key_rows, value_rows, out_weight, levels, owner_map):
    n = lax.axis_size("seq")
    outer = n // 4
    tokens_dev, width = queries.shape
    pairs = width // HD
    heads_dev = out_weight.shape[0] // HD
    model = out_weight.shape[1]
    tokens = tokens_dev * n
    keys = key_rows.shape[0]
    chunks = model // (SUB * HD)
    block_rows = tokens_dev * pairs + SUB

    cfg = (n, outer, tokens_dev, heads_dev, pairs, chunks)
    message = (heads_dev + 1, tokens, HD)
    vmem = pltpu.VMEM
    dma = pltpu.SemaphoreType.DMA
    return pl.pallas_call(
        functools.partial(kernel, cfg),
        out_shape=jax.ShapeDtypeStruct((tokens_dev, model), F32),
        in_specs=[pl.BlockSpec(memory_space=pl.ANY)] * 6,
        out_specs=pl.BlockSpec(memory_space=pltpu.VMEM),
        scratch_shapes=[
            vmem(key_rows.shape, BF16),
            vmem(value_rows.shape, BF16),
            vmem(out_weight.shape, BF16),
            vmem(queries.shape, BF16),
            vmem(levels.shape, jnp.int32),
            vmem(owner_map.shape, jnp.int32),
            vmem((block_rows, HD), F32),
            vmem((n, block_rows, HD), BF16),
            vmem((n * block_rows, HD), F32),
            vmem((pairs, tokens, HD), BF16),
            vmem((n // 2,) + message, BF16),
            vmem((n // 2,) + message, BF16),
            vmem((outer,) + message, BF16),
            vmem((outer,) + message, BF16),
            vmem((outer,) + message, BF16),
            vmem((outer,) + message, BF16),
            vmem((chunks, tokens * SUB, HD), F32),
            vmem((chunks, tokens * SUB, HD), BF16),
            vmem((chunks, tokens // 2 * SUB, HD), BF16),
            vmem((chunks, tokens // 4 * SUB, HD), BF16),
            vmem((chunks, tokens // 4 * SUB, HD), BF16),
            vmem((chunks, outer, tokens_dev * SUB, HD), BF16),
            vmem((chunks, outer, tokens_dev * SUB, HD), BF16),
            vmem((tokens_dev * SUB, HD), F32),
            dma((6,)),
            dma((2, 4 * outer)),
            dma((2, n)),
            dma((n // 2,)),
            dma((n // 2,)),
            dma((outer,)),
            dma((outer,)),
            dma((outer,)),
            dma((outer,)),
            dma((chunks,)),
            dma((chunks,)),
            dma((chunks,)),
            dma((chunks,)),
            dma((chunks, outer)),
            dma((chunks, outer)),
        ],
        compiler_params=pltpu.CompilerParams(
            collective_id=0, has_side_effects=True, vmem_limit_bytes=56 * 1024 * 1024
        ),
        cost_estimate=pl.CostEstimate(
            flops=4 * tokens * keys * width + 2 * tokens * heads_dev * HD * model,
            bytes_accessed=2 * (2 * keys * width + heads_dev * HD * model),
            transcendentals=tokens * keys * pairs,
        ),
    )(queries, key_rows, value_rows, out_weight, levels, owner_map).astype(BF16)


def solution(mesh):
    return jax.shard_map(
        on_device,
        mesh=mesh,
        in_specs=(
            P(("groups", "seq"), None),
            P(("groups", "seq"), None),
            P(("groups", "seq"), None),
            P("seq", None),
            P(None, ("groups", "seq")),
            P(None, ("groups", "seq")),
        ),
        out_specs=P(("groups", "seq"), None),
        check_vma=False,
    )
```

```python
import functools
import math

import jax
import jax.numpy as jnp
from jax import lax
from jax.experimental import pallas as pl
from jax.experimental.pallas import tpu as pltpu
from jax.sharding import PartitionSpec as P

HD = 128
HEADS = 16
CONTROLS = 3
LEVELS = 8
SUB = 16
PARTS = 4
MESH = pl.DeviceIdType.MESH
F32 = jnp.float32
BF16 = jnp.bfloat16


def kernel(
    cfg, q_hbm, k_hbm, v_hbm, w_hbm, level_hbm, owner_hbm, out_ref,
    k_ref, v_ref, w_ref, q_ref, level_ref, owner_ref, qs, qg, qf, qh,
    sb_core, rb_core, sb_y, rb_y, sb_z, rb_z,
    pf, pb, rc, sy, ry, sz, rz, done,
    load_sem, ag_send, ag_recv,
    core_s, core_r, y_s, y_r, z_s, z_r,
    pc_s, pc_r, py_s, py_r, pz_s, pz_r,
):
    n, outer, tokens_dev, heads_dev, pairs, chunks = cfg
    tokens = tokens_dev * n
    group = lax.axis_index("groups")
    me = lax.axis_index("seq")
    z, y, c = me // 4, (me // 2) % 2, me % 2

    def dev(zz, yy, cc):
        return (group, zz * 4 + yy * 2 + cc)

    sibling, across = dev(z, y, 1 - c), dev(z, 1 - y, c)

    loads = [
        pltpu.make_async_copy(src, dst, load_sem.at[i])
        for i, (src, dst) in enumerate(
            [
                (q_hbm, q_ref), (level_hbm, level_ref), (owner_hbm, owner_ref),
                (k_hbm, k_ref), (v_hbm, v_ref), (w_hbm, w_ref),
            ]
        )
    ]
    for load in loads[:5]:
        load.start()

    barrier = pltpu.get_barrier_semaphore()
    pl.semaphore_signal(barrier, inc=1, device_id=sibling, device_id_type=MESH)
    pl.semaphore_signal(barrier, inc=1, device_id=across, device_id_type=MESH)
    for step in range(1, outer):
        pl.semaphore_signal(
            barrier, inc=1, device_id=dev((z + step) % outer, y, c), device_id_type=MESH
        )

    def send(src, dst, s_sem, r_sem, target):
        return pltpu.make_async_remote_copy(
            src_ref=src, dst_ref=dst, send_sem=s_sem, recv_sem=r_sem,
            device_id=target, device_id_type=MESH,
        )

    part_heads = pairs // PARTS
    part_rows = tokens_dev * part_heads
    info_at = PARTS * part_rows
    block_rows = info_at + SUB
    for load in loads[:3]:
        load.wait()
    for h in range(pairs):
        first = h // part_heads * part_rows + h % part_heads
        qs[pl.ds(first, tokens_dev, stride=part_heads), :] = (
            q_ref[:, h * HD:(h + 1) * HD].astype(F32)
        )
    qs[info_at:, :] = jnp.zeros((SUB, HD), F32)
    qs[info_at:info_at + CONTROLS, 0:tokens_dev] = owner_ref[...].astype(F32)
    qs[info_at + 8:info_at + 8 + CONTROLS, 0:tokens_dev] = level_ref[...].astype(F32)
    qg[me] = qs[...].astype(BF16)
    qf[pl.ds(pl.multiple_of(me * block_rows, SUB), block_rows), :] = qs[...]

    pl.semaphore_wait(barrier, outer + 1)

    counts = [part_rows] * (PARTS - 1) + [part_rows + SUB]
    spans = [pl.ds(part * part_rows, count) for part, count in enumerate(counts)]

    def ag(part, block, slot, target):
        ref = qg.at[block, spans[part]]
        return send(ref, ref, ag_send.at[part, slot], ag_recv.at[part, block], target)

    def own_sends(part):
        for step in range(1, outer):
            ag(part, me, step, dev((z + step) % outer, y, c)).start()
        ag(part, me, outer, across).start()
        ag(part, me, 2 * outer, sibling).start()

    def widen(part, block):
        first = block * block_rows + part * part_rows
        count = counts[part]
        qf[pl.ds(pl.multiple_of(first, SUB), count), :] = qg[block, spans[part]].astype(F32)

    def from_z(part):
        for step in range(1, outer):
            block = ((z + step) % outer) * 4 + y * 2 + c
            ag(part, block, step, across).wait_recv()
            ag(part, block, outer + step, across).start()
            ag(part, block, 2 * outer + step, sibling).start()
            widen(part, block)

    def from_across(part, step):
        block = ((z + step) % outer) * 4 + (1 - y) * 2 + c
        ag(part, block, step, across).wait_recv()
        ag(part, block, 3 * outer + step, sibling).start()
        widen(part, block)

    def from_sibling(part):
        for yy in (y, 1 - y):
            for step in range(outer):
                block = ((z + step) % outer) * 4 + yy * 2 + (1 - c)
                ag(part, block, step, sibling).wait_recv()
                widen(part, block)
        for h in range(part_heads):
            qh[part * part_heads + h] = jnp.concatenate(
                [
                    qf[pl.ds(part * part_rows + r * part_heads + h, n, stride=block_rows), :]
                    for r in range(tokens_dev)
                ],
                axis=0,
            ).astype(BF16)

    own_sends(0)
    from_z(0)
    own_sends(1)
    for step in range(outer):
        from_across(0, step)
    from_z(1)
    own_sends(2)
    loads[5].start()
    from_sibling(0)
    loads[3].wait()
    loads[4].wait()

    log_scale = HD ** -0.5 * math.log2(math.e)
    lane = lax.broadcasted_iota(jnp.int32, (tokens, HD), 1)
    mid = HD // 2

    def attend(targets):
        heads = [t * heads_dev + j for t in targets for j in range(heads_dev)]
        cols = [pl.ds(pl.multiple_of(h * HD, HD), HD) for h in heads]
        count = len(heads)
        scores, expo = [None] * count, [None] * count
        peaks, totals, sums = [None] * count, [None] * count, [None] * count
        for step in range(count + 4):
            if step < count:
                scores[step] = lax.dot_general(
                    qh[heads[step]], k_ref[:, cols[step]], (((1,), (1,)), ((), ())),
                    preferred_element_type=F32,
                )
            i = step - 2
            if 0 <= i < count:
                peak = jnp.max(scores[i], axis=1, keepdims=True) * log_scale
                peaks[i] = peak.astype(BF16).astype(F32)
                p = jnp.exp2(scores[i] * log_scale - peaks[i])
                totals[i] = jnp.sum(p, axis=1, keepdims=True)
                expo[i] = p.astype(BF16)
                scores[i] = None
            i = step - 4
            if 0 <= i < count:
                sums[i] = jnp.dot(expo[i], v_ref[:, cols[i]], preferred_element_type=F32)
                expo[i] = None
        found = []
        for i in range(len(targets)):
            stat = jnp.zeros((tokens, HD), F32)
            for j in range(heads_dev):
                stat = jnp.where(lane == j, peaks[i * heads_dev + j], stat)
                stat = jnp.where(lane == mid + j, totals[i * heads_dev + j], stat)
            found.append((sums[i * heads_dev:(i + 1) * heads_dev], stat))
        return found

    def write(ref, found):
        sums, stat = found
        for j in range(heads_dev):
            ref[j] = sums[j].astype(BF16)
        ref[heads_dev] = stat.astype(BF16)

    def merge(found, refs):
        sums, stat = found
        stats = [stat] + [ref[heads_dev].astype(F32) for ref in refs]
        best = functools.reduce(jnp.maximum, stats)
        factors = [jnp.exp2(s - best) for s in stats]
        total = sum(s * pltpu.roll(f, mid, 1) for s, f in zip(stats, factors))
        merged = []
        for j in range(heads_dev):
            o = sums[j] * factors[0][:, j:j + 1]
            for ref, f in zip(refs, factors[1:]):
                o = o + ref[j].astype(F32) * f[:, j:j + 1]
            merged.append(o)
        return merged, jnp.where(lane < mid, best, total)

    def core_copy(slot):
        return send(sb_core.at[slot], rb_core.at[slot], core_s.at[slot], core_r.at[slot], sibling)

    def y_copy(zz):
        return send(sb_y.at[zz], rb_y.at[zz], y_s.at[zz], y_r.at[zz], across)

    def z_copy(zz, sender):
        return send(sb_z.at[zz], rb_z.at[sender], z_s.at[zz], z_r.at[sender], dev(zz, y, c))

    def sibling_slots(zz):
        slots = [zz * 2 + 1 - y, zz * 2 + y]
        for slot, found in zip(slots, attend([slot * 2 + 1 - c for slot in slots])):
            write(sb_core.at[slot], found)
            core_copy(slot).start()

    part_zs = outer // PARTS
    for part in range(PARTS):
        if part + 1 < PARTS:
            for step in range(outer):
                from_across(part + 1, step)
        if part + 2 < PARTS:
            from_z(part + 2)
        if part + 3 < PARTS:
            own_sends(part + 3)

        def of_part(i, carry):
            sibling_slots(part * part_zs + i)
            return carry

        lax.fori_loop(0, part_zs, of_part, 0)
        if part + 1 < PARTS:
            from_sibling(part + 1)

    def for_across(i, carry):
        zs = [(z + 1 + 2 * i) % outer, (z + 2 + 2 * i) % outer]
        slots = [zz * 2 + 1 - y for zz in zs]
        both = attend([slot * 2 + c for slot in slots])
        for zz, slot, found in zip(zs, slots, both):
            core_copy(slot).wait_recv()
            write(sb_y.at[zz], merge(found, [rb_core.at[slot]]))
            y_copy(zz).start()
        return carry

    lax.fori_loop(0, outer // 2, for_across, 0)

    def collect(zz, found):
        slot = zz * 2 + y
        core_copy(slot).wait_recv()
        y_copy(zz).wait_recv()
        return merge(found, [rb_core.at[slot], rb_y.at[zz]])

    def for_z(i, carry):
        zs = [(z + 1 + 2 * i) % outer, (z + 2 + 2 * i) % outer]
        for zz, found in zip(zs, attend([zz * 4 + y * 2 + c for zz in zs])):
            write(sb_z.at[zz], collect(zz, found))
            z_copy(zz, z).start()
        return carry

    lax.fori_loop(0, outer // 2 - 1, for_z, 0)
    final = (z + outer - 1) % outer
    found, mine = attend([final * 4 + y * 2 + c, me])
    write(sb_z.at[final], collect(final, found))
    z_copy(final, z).start()
    mine = collect(z, mine)

    section = me * heads_dev // HEADS

    def column(first):
        rows = jnp.zeros((n, HD), F32)
        for s in range(CONTROLS):
            found_rows = qf[pl.ds(info_at + first + s, n, stride=block_rows), :]
            rows = jnp.where(section == s, found_rows, rows)
        return jnp.concatenate([rows[:, r:r + 1] for r in range(tokens_dev)], axis=0)

    position = lax.broadcasted_iota(jnp.int32, (n, 1), 0) * tokens_dev
    position = jnp.concatenate([position + r for r in range(tokens_dev)], axis=0).astype(F32)
    is_base = section >= CONTROLS
    owner = jnp.where(is_base, position, column(0))
    level = jnp.where(is_base, float(LEVELS), column(8))
    holder = jnp.floor((owner + 0.5) * (1.0 / tokens_dev))
    chip = jnp.floor(holder * 0.5)
    z_of = jnp.floor(holder * 0.25)
    order = (holder - 2 * chip) * (n // 2) + (chip - 2 * z_of) * outer + z_of
    place = order * tokens_dev + owner - holder * tokens_dev
    picked = lax.broadcasted_iota(jnp.int32, (tokens, tokens), 1) == place.astype(jnp.int32)
    picked = picked.astype(F32).T.astype(BF16)
    level = jnp.broadcast_to(level, (tokens, HD)).astype(BF16)
    row_weight = jnp.dot(picked, level, preferred_element_type=F32)[:, 0:1] / LEVELS

    for step in range(1, outer):
        z_copy((z + step) % outer, (z + step) % outer).wait_recv()
    sums, stat = merge(mine, [rb_z.at[(z + step) % outer] for step in range(1, outer)])
    attended = jnp.concatenate(
        [(sums[j] / stat[:, mid + j:mid + j + 1]).astype(BF16) for j in range(heads_dev)], axis=1
    )
    chosen = jnp.dot(picked, attended, preferred_element_type=F32).astype(BF16)

    loads[5].wait()
    half, quarter, piece = tokens // 2 * SUB, tokens // 4 * SUB, tokens_dev * SUB

    def rows_at(first, count):
        return pl.ds(pl.multiple_of(first, SUB), count)

    def pc_copy(cc):
        rows = rows_at((1 - c) * half, half)
        return send(pb.at[cc, rows], rc.at[cc], pc_s.at[cc], pc_r.at[cc], sibling)

    def py_copy(cc):
        return send(sy.at[cc], ry.at[cc], py_s.at[cc], py_r.at[cc], across)

    def pz_copy(cc, zz, sender):
        return send(
            sz.at[cc, zz], rz.at[cc, sender], pz_s.at[cc, zz], pz_r.at[cc, sender], dev(zz, y, c)
        )

    width = 4 * HD
    for cc in range(chunks):
        for g in range(SUB * HD // width):
            first = cc * SUB * HD + g * width
            product = jnp.dot(
                chosen, w_ref[:, first:first + width], preferred_element_type=F32
            ) * row_weight
            for t in range(width // HD):
                pf[cc, pl.ds(g * (width // HD) + t, tokens, stride=SUB), :] = (
                    product[:, t * HD:(t + 1) * HD]
                )
        rows = rows_at((1 - c) * half, half)
        pb[cc, rows] = pf[cc, rows].astype(BF16)
        pc_copy(cc).start()

    for cc in range(chunks):
        pc_copy(cc).wait_recv()
        away, near = rows_at((1 - y) * quarter, quarter), rows_at(y * quarter, quarter)
        away_own = rows_at(c * half + (1 - y) * quarter, quarter)
        sy[cc] = (pf[cc, away_own] + rc[cc, away].astype(F32)).astype(BF16)
        py_copy(cc).start()
    for cc in range(chunks):
        py_copy(cc).wait_recv()
        for step in range(1, outer):
            zz = (z + step) % outer
            own = rows_at(c * half + y * quarter + zz * piece, piece)
            from_core = rows_at(y * quarter + zz * piece, piece)
            from_y = rows_at(zz * piece, piece)
            sz[cc, zz] = (
                pf[cc, own] + rc[cc, from_core].astype(F32) + ry[cc, from_y].astype(F32)
            ).astype(BF16)
            pz_copy(cc, zz, z).start()
    for cc in range(chunks):
        own = rows_at(c * half + y * quarter + z * piece, piece)
        from_core = rows_at(y * quarter + z * piece, piece)
        from_y = rows_at(z * piece, piece)
        total = pf[cc, own] + rc[cc, from_core].astype(F32) + ry[cc, from_y].astype(F32)
        for step in range(1, outer):
            sender = (z + step) % outer
            pz_copy(cc, sender, sender).wait_recv()
            total = total + rz[cc, sender].astype(F32)
        done[...] = total
        for t in range(SUB):
            out_ref[:, (cc * SUB + t) * HD:(cc * SUB + t + 1) * HD] = (
                done[pl.ds(t, tokens_dev, stride=SUB), :].astype(BF16)
            )

    for part in range(PARTS):
        for slot in range(1, 4 * outer):
            ag(part, me, slot, across).wait_send()
    for slot in range(2 * outer):
        core_copy(slot).wait_send()
    for zz in range(outer):
        y_copy(zz).wait_send()
    for step in range(1, outer):
        z_copy((z + step) % outer, z).wait_send()
    for cc in range(chunks):
        pc_copy(cc).wait_send()
        py_copy(cc).wait_send()
        for step in range(1, outer):
            pz_copy(cc, (z + step) % outer, z).wait_send()


def on_device(queries, key_rows, value_rows, out_weight, levels, owner_map):
    n = lax.axis_size("seq")
    outer = n // 4
    tokens_dev, width = queries.shape
    pairs = width // HD
    heads_dev = out_weight.shape[0] // HD
    model = out_weight.shape[1]
    tokens = tokens_dev * n
    keys = key_rows.shape[0]
    chunks = model // (SUB * HD)
    block_rows = tokens_dev * pairs + SUB

    cfg = (n, outer, tokens_dev, heads_dev, pairs, chunks)
    message = (heads_dev + 1, tokens, HD)
    vmem = pltpu.VMEM
    dma = pltpu.SemaphoreType.DMA
    return pl.pallas_call(
        functools.partial(kernel, cfg),
        out_shape=jax.ShapeDtypeStruct((tokens_dev, model), BF16),
        in_specs=[pl.BlockSpec(memory_space=pl.ANY)] * 6,
        out_specs=pl.BlockSpec(memory_space=pltpu.VMEM),
        scratch_shapes=[
            vmem(key_rows.shape, BF16),
            vmem(value_rows.shape, BF16),
            vmem(out_weight.shape, BF16),
            vmem(queries.shape, BF16),
            vmem(levels.shape, jnp.int32),
            vmem(owner_map.shape, jnp.int32),
            vmem((block_rows, HD), F32),
            vmem((n, block_rows, HD), BF16),
            vmem((n * block_rows, HD), F32),
            vmem((pairs, tokens, HD), BF16),
            vmem((n // 2,) + message, BF16),
            vmem((n // 2,) + message, BF16),
            vmem((outer,) + message, BF16),
            vmem((outer,) + message, BF16),
            vmem((outer,) + message, BF16),
            vmem((outer,) + message, BF16),
            vmem((chunks, tokens * SUB, HD), F32),
            vmem((chunks, tokens * SUB, HD), BF16),
            vmem((chunks, tokens // 2 * SUB, HD), BF16),
            vmem((chunks, tokens // 4 * SUB, HD), BF16),
            vmem((chunks, tokens // 4 * SUB, HD), BF16),
            vmem((chunks, outer, tokens_dev * SUB, HD), BF16),
            vmem((chunks, outer, tokens_dev * SUB, HD), BF16),
            vmem((tokens_dev * SUB, HD), F32),
            dma((6,)),
            dma((PARTS, 4 * outer)),
            dma((PARTS, n)),
            dma((n // 2,)),
            dma((n // 2,)),
            dma((outer,)),
            dma((outer,)),
            dma((outer,)),
            dma((outer,)),
            dma((chunks,)),
            dma((chunks,)),
            dma((chunks,)),
            dma((chunks,)),
            dma((chunks, outer)),
            dma((chunks, outer)),
        ],
        compiler_params=pltpu.CompilerParams(
            collective_id=0, has_side_effects=True, vmem_limit_bytes=56 * 1024 * 1024
        ),
        cost_estimate=pl.CostEstimate(
            flops=4 * tokens * keys * width + 2 * tokens * heads_dev * HD * model,
            bytes_accessed=2 * (2 * keys * width + heads_dev * HD * model),
            transcendentals=tokens * keys * pairs,
        ),
    )(queries, key_rows, value_rows, out_weight, levels, owner_map)


def solution(mesh):
    return jax.shard_map(
        on_device,
        mesh=mesh,
        in_specs=(
            P(("groups", "seq"), None),
            P(("groups", "seq"), None),
            P(("groups", "seq"), None),
            P("seq", None),
            P(None, ("groups", "seq")),
            P(None, ("groups", "seq")),
        ),
        out_specs=P(("groups", "seq"), None),
        check_vma=False,
    )
```

```python
import functools
import math

import jax
import jax.numpy as jnp
from jax import lax
from jax.experimental import pallas as pl
from jax.experimental.pallas import tpu as pltpu
from jax.sharding import PartitionSpec as P

HD = 128
HEADS = 16
CONTROLS = 3
LEVELS = 8
SUB = 16
MESH = pl.DeviceIdType.MESH
F32 = jnp.float32
BF16 = jnp.bfloat16


def kernel(
    cfg, q_hbm, k_hbm, v_hbm, w_hbm, level_hbm, owner_hbm, out_ref,
    k_ref, v_ref, w_ref, q_ref, level_ref, owner_ref, qs, qg0, qg1, qf, qh,
    sb_core, rb_core, sb_y, rb_y, sb_z, rb_z,
    pf, pb, rc, sp, rp, done,
    load_sem, ag_send, ag_recv,
    core_s, core_r, y_s, y_r, z_s, z_r,
    pc_s, pc_r, p_s, p_r,
):
    n, outer, tokens_dev, heads_dev, pairs, chunks = cfg
    tokens = tokens_dev * n
    group = lax.axis_index("groups")
    me = lax.axis_index("seq")
    z, low = lax.div(me, 4), lax.rem(me, 4)
    y, c = lax.div(low, 2), lax.rem(low, 2)
    zs = [lax.rem(z + step, outer) for step in range(1, outer)] + [z]

    def dev(zz, yy, cc):
        return (group, zz * 4 + yy * 2 + cc)

    sibling, across = dev(z, y, 1 - c), dev(z, 1 - y, c)

    loads = [
        pltpu.make_async_copy(src, dst, load_sem.at[i])
        for i, (src, dst) in enumerate(
            [
                (q_hbm, q_ref), (level_hbm, level_ref), (owner_hbm, owner_ref),
                (k_hbm, k_ref), (v_hbm, v_ref), (w_hbm, w_ref),
            ]
        )
    ]
    for load in loads[:5]:
        load.start()

    barrier = pltpu.get_barrier_semaphore()
    pl.semaphore_signal(barrier, inc=1, device_id=sibling, device_id_type=MESH)
    pl.semaphore_signal(barrier, inc=1, device_id=across, device_id_type=MESH)
    for zz in zs[:-1]:
        for yy in (y, 1 - y):
            pl.semaphore_signal(
                barrier, inc=1, device_id=dev(zz, yy, c), device_id_type=MESH
            )

    def send(src, dst, s_sem, r_sem, target):
        return pltpu.make_async_remote_copy(
            src_ref=src, dst_ref=dst, send_sem=s_sem, recv_sem=r_sem,
            device_id=target, device_id_type=MESH,
        )

    part_heads = pairs // 2
    part_rows = tokens_dev * part_heads
    block_rows = 2 * part_rows + SUB
    for load in loads[:3]:
        load.wait()
    for h in range(pairs):
        first = h // part_heads * part_rows + h % part_heads
        qs[pl.ds(first, tokens_dev, stride=part_heads), :] = (
            q_ref[:, h * HD:(h + 1) * HD].astype(F32)
        )
    qs[2 * part_rows:, :] = jnp.zeros((SUB, HD), F32)
    qs[2 * part_rows:2 * part_rows + CONTROLS, 0:tokens_dev] = owner_ref[...].astype(F32)
    qs[2 * part_rows + 8:2 * part_rows + 8 + CONTROLS, 0:tokens_dev] = level_ref[...].astype(F32)
    place_of = (y * 2 + c) * outer
    mine_at = place_of + z
    qg0[mine_at] = qs[0:part_rows, :].astype(BF16)
    qg1[mine_at] = qs[part_rows:, :].astype(BF16)
    qf[pl.ds(pl.multiple_of(mine_at * block_rows, SUB), block_rows), :] = qs[...]

    pl.semaphore_wait(barrier, 2 * outer)

    parts = (qg0, qg1)
    across_at = ((1 - y) * 2 + c) * outer

    def along(part, target_z, sender_z):
        ref = parts[part].at[mine_at]
        return send(
            ref, ref, ag_send.at[part, target_z], ag_recv.at[part, sender_z], dev(target_z, y, c)
        )

    def cross(part, zz):
        ref = parts[part].at[place_of + zz]
        return send(ref, ref, ag_send.at[part, outer + zz], ag_recv.at[part, outer + zz], across)

    def hand(part, second):
        ref = parts[part].at[pl.ds(across_at if second else place_of, outer)]
        slot = 2 * outer + second
        return send(ref, ref, ag_send.at[part, slot], ag_recv.at[part, slot], sibling)

    for part in range(2):
        for zz in zs[:-1]:
            along(part, zz, z).start()
        cross(part, z).start()

    def widen(part, block):
        first = block * block_rows + part * part_rows
        count = part_rows + part * SUB
        qf[pl.ds(pl.multiple_of(first, SUB), count), :] = parts[part][block].astype(F32)

    def from_z(part):
        for zz in zs[:-1]:
            along(part, zz, zz).wait_recv()
            cross(part, zz).start()
        hand(part, 0).start()
        for zz in zs[:-1]:
            widen(part, place_of + zz)

    def from_across(part):
        for zz in zs[-1:] + zs[:-1]:
            cross(part, zz).wait_recv()
        hand(part, 1).start()
        for zz in zs:
            widen(part, across_at + zz)

    def from_sibling(part):
        for second, yy in ((0, y), (1, 1 - y)):
            hand(part, second).wait_recv()
            for zz in range(outer):
                widen(part, (yy * 2 + 1 - c) * outer + zz)
        for h in range(part_heads):
            qh[part * part_heads + h] = jnp.concatenate(
                [
                    qf[pl.ds(part * part_rows + r * part_heads + h, n, stride=block_rows), :]
                    for r in range(tokens_dev)
                ],
                axis=0,
            ).astype(BF16)

    from_z(0)
    from_across(0)
    from_z(1)
    loads[5].start()
    from_sibling(0)
    loads[3].wait()
    loads[4].wait()

    log_scale = HD ** -0.5 * math.log2(math.e)
    lane = lax.broadcasted_iota(jnp.int32, (tokens, HD), 1)
    mid = HD // 2

    def attend(targets):
        heads = [t * heads_dev + j for t in targets for j in range(heads_dev)]
        cols = [pl.ds(pl.multiple_of(h * HD, HD), HD) for h in heads]
        scores = [
            lax.dot_general(
                qh[h], k_ref[:, col], (((1,), (1,)), ((), ())), preferred_element_type=F32
            ) * log_scale
            for h, col in zip(heads, cols)
        ]
        peaks = [jnp.max(s, axis=1, keepdims=True).astype(BF16).astype(F32) for s in scores]
        expo = [jnp.exp2(s - m) for s, m in zip(scores, peaks)]
        totals = [jnp.sum(p, axis=1, keepdims=True) for p in expo]
        sums = [
            jnp.dot(p.astype(BF16), v_ref[:, col], preferred_element_type=F32)
            for p, col in zip(expo, cols)
        ]
        found = []
        for i in range(len(targets)):
            stat = jnp.zeros((tokens, HD), F32)
            for j in range(heads_dev):
                stat = jnp.where(lane == j, peaks[i * heads_dev + j], stat)
                stat = jnp.where(lane == mid + j, totals[i * heads_dev + j], stat)
            found.append((sums[i * heads_dev:(i + 1) * heads_dev], stat))
        return found

    def write(ref, found):
        sums, stat = found
        for j in range(heads_dev):
            ref[j] = sums[j].astype(BF16)
        ref[heads_dev] = stat.astype(BF16)

    def merge(found, refs):
        sums, stat = found
        stats = [stat] + [ref[heads_dev].astype(F32) for ref in refs]
        best = functools.reduce(jnp.maximum, stats)
        factors = [jnp.exp2(s - best) for s in stats]
        total = sum(s * pltpu.roll(f, mid, 1) for s, f in zip(stats, factors))
        merged = []
        for j in range(heads_dev):
            o = sums[j] * factors[0][:, j:j + 1]
            for ref, f in zip(refs, factors[1:]):
                o = o + ref[j].astype(F32) * f[:, j:j + 1]
            merged.append(o)
        return merged, jnp.where(lane < mid, best, total)

    def core_copy(slot):
        return send(sb_core.at[slot], rb_core.at[slot], core_s.at[slot], core_r.at[slot], sibling)

    def y_copy(zz):
        return send(sb_y.at[zz], rb_y.at[zz], y_s.at[zz], y_r.at[zz], across)

    def z_copy(zz, sender):
        return send(sb_z.at[zz], rb_z.at[sender], z_s.at[zz], z_r.at[sender], dev(zz, y, c))

    def sibling_slots(zz):
        slots = [zz * 2 + 1 - y, zz * 2 + y]
        for slot, found in zip(slots, attend([slot * 2 + 1 - c for slot in slots])):
            write(sb_core.at[slot], found)
            core_copy(slot).start()

    def sibling_step(i, carry):
        sibling_slots(i)
        return carry

    lax.fori_loop(0, outer // 4, sibling_step, 0)
    from_across(1)
    lax.fori_loop(outer // 4, outer // 2, sibling_step, 0)
    from_sibling(1)
    lax.fori_loop(outer // 2, outer, sibling_step, 0)

    def for_across(i, carry):
        pair = [lax.rem(z + 1 + 2 * i, outer), lax.rem(z + 2 + 2 * i, outer)]
        slots = [zz * 2 + 1 - y for zz in pair]
        both = attend([slot * 2 + c for slot in slots])
        for zz, slot, found in zip(pair, slots, both):
            core_copy(slot).wait_recv()
            write(sb_y.at[zz], merge(found, [rb_core.at[slot]]))
            y_copy(zz).start()
        return carry

    lax.fori_loop(0, outer // 2, for_across, 0)

    def collect(zz, found):
        slot = zz * 2 + y
        core_copy(slot).wait_recv()
        y_copy(zz).wait_recv()
        return merge(found, [rb_core.at[slot], rb_y.at[zz]])

    def for_z(i, carry):
        pair = [lax.rem(z + 1 + 2 * i, outer), lax.rem(z + 2 + 2 * i, outer)]
        for zz, found in zip(pair, attend([zz * 4 + y * 2 + c for zz in pair])):
            write(sb_z.at[zz], collect(zz, found))
            z_copy(zz, z).start()
        return carry

    lax.fori_loop(0, outer // 2 - 1, for_z, 0)
    final = zs[-2]
    found, mine = attend([final * 4 + y * 2 + c, me])
    write(sb_z.at[final], collect(final, found))
    z_copy(final, z).start()
    mine = collect(z, mine)

    section = lax.div(me * heads_dev, HEADS)

    def column(first):
        rows = jnp.zeros((n, HD), F32)
        for s in range(CONTROLS):
            found_rows = qf[pl.ds(2 * part_rows + first + s, n, stride=block_rows), :]
            rows = jnp.where(section == s, found_rows, rows)
        return jnp.concatenate([rows[:, r:r + 1] for r in range(tokens_dev)], axis=0)

    block = lax.broadcasted_iota(jnp.int32, (n, 1), 0).astype(F32)
    line = jnp.floor((block + 0.5) * (1.0 / outer))
    position = ((block - line * outer) * 4 + line) * tokens_dev
    position = jnp.concatenate([position + r for r in range(tokens_dev)], axis=0)
    is_base = section >= CONTROLS
    owner = jnp.where(is_base, position, column(0))
    level = jnp.where(is_base, float(LEVELS), column(8))
    holder = jnp.floor((owner + 0.5) * (1.0 / tokens_dev))
    chip = jnp.floor(holder * 0.5)
    z_of = jnp.floor(holder * 0.25)
    order = (holder - 2 * chip) * (n // 2) + (chip - 2 * z_of) * outer + z_of
    place = order * tokens_dev + owner - holder * tokens_dev
    picked = lax.broadcasted_iota(jnp.int32, (tokens, tokens), 1) == place.astype(jnp.int32)
    picked = picked.astype(F32).T.astype(BF16)
    level = jnp.broadcast_to(level, (tokens, HD)).astype(BF16)
    row_weight = jnp.dot(picked, level, preferred_element_type=F32)[:, 0:1] / LEVELS

    for zz in zs[:-1]:
        z_copy(zz, zz).wait_recv()
    sums, stat = merge(mine, [rb_z.at[zz] for zz in zs[:-1]])
    attended = jnp.concatenate(
        [(sums[j] / stat[:, mid + j:mid + j + 1]).astype(BF16) for j in range(heads_dev)], axis=1
    )
    chosen = jnp.dot(picked, attended, preferred_element_type=F32).astype(BF16)

    loads[5].wait()
    half, piece = tokens // 2 * SUB, tokens_dev * SUB

    def rows_at(first, count):
        return pl.ds(pl.multiple_of(first, SUB), count)

    def pc_copy(cc):
        rows = rows_at((1 - c) * half, half)
        return send(pb.at[cc, rows], rc.at[cc], pc_s.at[cc], pc_r.at[cc], sibling)

    def p_copy(zz, yy, sender_z, sender_y):
        return send(
            sp.at[yy * outer + zz], rp.at[sender_y * outer + sender_z],
            p_s.at[yy * outer + zz], p_r.at[sender_y * outer + sender_z], dev(zz, yy, c),
        )

    width = 4 * HD
    for cc in range(chunks):
        for g in range(SUB * HD // width):
            first = cc * SUB * HD + g * width
            product = jnp.dot(
                chosen, w_ref[:, first:first + width], preferred_element_type=F32
            ) * row_weight
            for t in range(width // HD):
                pf[cc, pl.ds(g * (width // HD) + t, tokens, stride=SUB), :] = (
                    product[:, t * HD:(t + 1) * HD]
                )
        rows = rows_at((1 - c) * half, half)
        pb[cc, rows] = pf[cc, rows].astype(BF16)
        pc_copy(cc).start()

    for cc in range(chunks):
        pc_copy(cc).wait_recv()

    def partial_sum(cc, zz, yy):
        at = (yy * outer + zz) * piece
        return pf[cc, rows_at(c * half + at, piece)] + rc[cc, rows_at(at, piece)].astype(F32)

    peers = [(zz, yy) for zz in zs[:-1] for yy in (1 - y, y)] + [(z, 1 - y)]
    for zz, yy in peers:
        for cc in range(chunks):
            sp[yy * outer + zz, cc] = partial_sum(cc, zz, yy).astype(BF16)
        p_copy(zz, yy, z, y).start()
    totals = [partial_sum(cc, z, y) for cc in range(chunks)]
    for zz, yy in peers:
        p_copy(zz, yy, zz, yy).wait_recv()
    for cc in range(chunks):
        total = totals[cc]
        for zz, yy in peers:
            total = total + rp[yy * outer + zz, cc].astype(F32)
        done[...] = total
        for t in range(SUB):
            out_ref[:, (cc * SUB + t) * HD:(cc * SUB + t + 1) * HD] = (
                done[pl.ds(t, tokens_dev, stride=SUB), :].astype(BF16)
            )

    for part in range(2):
        for zz in zs[:-1]:
            along(part, zz, z).wait_send()
        for zz in range(outer):
            cross(part, zz).wait_send()
        hand(part, 0).wait_send()
        hand(part, 1).wait_send()
    for slot in range(2 * outer):
        core_copy(slot).wait_send()
    for zz in range(outer):
        y_copy(zz).wait_send()
    for zz in zs[:-1]:
        z_copy(zz, z).wait_send()
    for cc in range(chunks):
        pc_copy(cc).wait_send()
    for zz, yy in peers:
        p_copy(zz, yy, z, y).wait_send()


def on_device(queries, key_rows, value_rows, out_weight, levels, owner_map):
    n = lax.axis_size("seq")
    outer = n // 4
    tokens_dev, width = queries.shape
    pairs = width // HD
    heads_dev = out_weight.shape[0] // HD
    model = out_weight.shape[1]
    tokens = tokens_dev * n
    keys = key_rows.shape[0]
    chunks = model // (SUB * HD)
    block_rows = tokens_dev * pairs + SUB

    cfg = (n, outer, tokens_dev, heads_dev, pairs, chunks)
    message = (heads_dev + 1, tokens, HD)
    vmem = pltpu.VMEM
    dma = pltpu.SemaphoreType.DMA
    return pl.pallas_call(
        functools.partial(kernel, cfg),
        out_shape=jax.ShapeDtypeStruct((tokens_dev, model), BF16),
        in_specs=[pl.BlockSpec(memory_space=pl.ANY)] * 6,
        out_specs=pl.BlockSpec(memory_space=pltpu.VMEM),
        scratch_shapes=[
            vmem(key_rows.shape, BF16),
            vmem(value_rows.shape, BF16),
            vmem(out_weight.shape, BF16),
            vmem(queries.shape, BF16),
            vmem(levels.shape, jnp.int32),
            vmem(owner_map.shape, jnp.int32),
            vmem((block_rows, HD), F32),
            vmem((n, block_rows // 2 - SUB // 2, HD), BF16),
            vmem((n, block_rows // 2 + SUB // 2, HD), BF16),
            vmem((n * block_rows, HD), F32),
            vmem((pairs, tokens, HD), BF16),
            vmem((n // 2,) + message, BF16),
            vmem((n // 2,) + message, BF16),
            vmem((outer,) + message, BF16),
            vmem((outer,) + message, BF16),
            vmem((outer,) + message, BF16),
            vmem((outer,) + message, BF16),
            vmem((chunks, tokens * SUB, HD), F32),
            vmem((chunks, tokens * SUB, HD), BF16),
            vmem((chunks, tokens // 2 * SUB, HD), BF16),
            vmem((2 * outer, chunks, tokens_dev * SUB, HD), BF16),
            vmem((2 * outer, chunks, tokens_dev * SUB, HD), BF16),
            vmem((tokens_dev * SUB, HD), F32),
            dma((6,)),
            dma((2, 2 * outer + 2)),
            dma((2, 2 * outer + 2)),
            dma((n // 2,)),
            dma((n // 2,)),
            dma((outer,)),
            dma((outer,)),
            dma((outer,)),
            dma((outer,)),
            dma((chunks,)),
            dma((chunks,)),
            dma((2 * outer,)),
            dma((2 * outer,)),
        ],
        compiler_params=pltpu.CompilerParams(
            collective_id=0, has_side_effects=True, vmem_limit_bytes=56 * 1024 * 1024
        ),
        cost_estimate=pl.CostEstimate(
            flops=4 * tokens * keys * width + 2 * tokens * heads_dev * HD * model,
            bytes_accessed=2 * (2 * keys * width + heads_dev * HD * model),
            transcendentals=tokens * keys * pairs,
        ),
    )(queries, key_rows, value_rows, out_weight, levels, owner_map)


def solution(mesh):
    return jax.shard_map(
        on_device,
        mesh=mesh,
        in_specs=(
            P(("groups", "seq"), None),
            P(("groups", "seq"), None),
            P(("groups", "seq"), None),
            P("seq", None),
            P(None, ("groups", "seq")),
            P(None, ("groups", "seq")),
        ),
        out_specs=P(("groups", "seq"), None),
        check_vma=False,
    )
```

```python
import functools
import math

import jax
import jax.numpy as jnp
from jax import lax
from jax.experimental import pallas as pl
from jax.experimental.pallas import tpu as pltpu
from jax.sharding import PartitionSpec as P

HD = 128
HEADS = 16
CONTROLS = 3
LEVELS = 8
SUB = 16
MESH = pl.DeviceIdType.MESH
F32 = jnp.float32
BF16 = jnp.bfloat16


def kernel(
    cfg, q_hbm, k_hbm, v_hbm, w_hbm, level_hbm, owner_hbm, out_ref,
    k_ref, v_ref, w_ref, q_ref, level_ref, owner_ref, qs, qg0, qg1, qf, qh,
    sb_core, rb_core, sb_y, rb_y, sb_z, rb_z,
    pf, pb, rc, sp, rp, done,
    load_sem, ag_send, ag_recv,
    core_s, core_r, y_s, y_r, z_s, z_r,
    pc_s, pc_r, p_s, p_r,
):
    n, outer, tokens_dev, heads_dev, pairs, chunks = cfg
    tokens = tokens_dev * n
    group = lax.axis_index("groups")
    me = lax.axis_index("seq")
    z, low = lax.div(me, 4), lax.rem(me, 4)
    y, c = lax.div(low, 2), lax.rem(low, 2)
    zs = [lax.rem(z + step, outer) for step in range(1, outer)] + [z]

    def dev(zz, yy, cc):
        return (group, zz * 4 + yy * 2 + cc)

    sibling, across = dev(z, y, 1 - c), dev(z, 1 - y, c)

    loads = [
        pltpu.make_async_copy(src, dst, load_sem.at[i])
        for i, (src, dst) in enumerate(
            [
                (q_hbm, q_ref), (level_hbm, level_ref), (owner_hbm, owner_ref),
                (k_hbm, k_ref), (v_hbm, v_ref), (w_hbm, w_ref),
            ]
        )
    ]
    for load in loads[:5]:
        load.start()

    barrier = pltpu.get_barrier_semaphore()
    pl.semaphore_signal(barrier, inc=1, device_id=sibling, device_id_type=MESH)
    pl.semaphore_signal(barrier, inc=1, device_id=across, device_id_type=MESH)
    for zz in zs[:-1]:
        for yy in (y, 1 - y):
            pl.semaphore_signal(
                barrier, inc=1, device_id=dev(zz, yy, c), device_id_type=MESH
            )

    def send(src, dst, s_sem, r_sem, target):
        return pltpu.make_async_remote_copy(
            src_ref=src, dst_ref=dst, send_sem=s_sem, recv_sem=r_sem,
            device_id=target, device_id_type=MESH,
        )

    part_heads = pairs // 2
    part_rows = tokens_dev * part_heads
    block_rows = 2 * part_rows + SUB
    for load in loads[:3]:
        load.wait()
    for h in range(pairs):
        first = h // part_heads * part_rows + h % part_heads
        qs[pl.ds(first, tokens_dev, stride=part_heads), :] = (
            q_ref[:, h * HD:(h + 1) * HD].astype(F32)
        )
    qs[2 * part_rows:, :] = jnp.zeros((SUB, HD), F32)
    qs[2 * part_rows:2 * part_rows + CONTROLS, 0:tokens_dev] = owner_ref[...].astype(F32)
    qs[2 * part_rows + 8:2 * part_rows + 8 + CONTROLS, 0:tokens_dev] = level_ref[...].astype(F32)
    place_of = (y * 2 + c) * outer
    mine_at = place_of + z
    qg0[mine_at] = qs[0:part_rows, :].astype(BF16)
    qg1[mine_at] = qs[part_rows:, :].astype(BF16)
    qf[pl.ds(pl.multiple_of(mine_at * block_rows, SUB), block_rows), :] = qs[...]

    pl.semaphore_wait(barrier, 2 * outer)

    parts = (qg0, qg1)
    across_at = ((1 - y) * 2 + c) * outer

    def along(part, target_z, sender_z):
        ref = parts[part].at[mine_at]
        return send(
            ref, ref, ag_send.at[part, target_z], ag_recv.at[part, sender_z], dev(target_z, y, c)
        )

    def cross(part, zz):
        ref = parts[part].at[place_of + zz]
        return send(ref, ref, ag_send.at[part, outer + zz], ag_recv.at[part, outer + zz], across)

    def hand(part, second):
        ref = parts[part].at[pl.ds(across_at if second else place_of, outer)]
        slot = 2 * outer + second
        return send(ref, ref, ag_send.at[part, slot], ag_recv.at[part, slot], sibling)

    for part in range(2):
        for zz in zs[:-1]:
            along(part, zz, z).start()
        cross(part, z).start()

    def widen(part, block):
        first = block * block_rows + part * part_rows
        count = part_rows + part * SUB
        qf[pl.ds(pl.multiple_of(first, SUB), count), :] = parts[part][block].astype(F32)

    def from_z(part):
        for zz in zs[:-1]:
            along(part, zz, zz).wait_recv()
            cross(part, zz).start()
        hand(part, 0).start()
        for zz in zs[:-1]:
            widen(part, place_of + zz)

    def from_across(part):
        for zz in zs[-1:] + zs[:-1]:
            cross(part, zz).wait_recv()
        hand(part, 1).start()
        for zz in zs:
            widen(part, across_at + zz)

    def from_sibling(part):
        for second, yy in ((0, y), (1, 1 - y)):
            hand(part, second).wait_recv()
            for zz in range(outer):
                widen(part, (yy * 2 + 1 - c) * outer + zz)
        for h in range(part_heads):
            qh[part * part_heads + h] = jnp.concatenate(
                [
                    qf[pl.ds(part * part_rows + r * part_heads + h, n, stride=block_rows), :]
                    for r in range(tokens_dev)
                ],
                axis=0,
            ).astype(BF16)

    from_z(0)
    from_across(0)
    from_z(1)
    loads[5].start()
    from_sibling(0)
    loads[3].wait()
    loads[4].wait()

    log_scale = HD ** -0.5 * math.log2(math.e)
    lane = lax.broadcasted_iota(jnp.int32, (tokens, HD), 1)
    mid = HD // 2

    def attend(targets):
        heads = [t * heads_dev + j for t in targets for j in range(heads_dev)]
        cols = [pl.ds(pl.multiple_of(h * HD, HD), HD) for h in heads]
        scores = [
            lax.dot_general(
                qh[h], k_ref[:, col], (((1,), (1,)), ((), ())), preferred_element_type=F32
            ) * log_scale
            for h, col in zip(heads, cols)
        ]
        peaks = [jnp.max(s, axis=1, keepdims=True).astype(BF16).astype(F32) for s in scores]
        expo = [jnp.exp2(s - m) for s, m in zip(scores, peaks)]
        totals = [jnp.sum(p, axis=1, keepdims=True) for p in expo]
        sums = [
            jnp.dot(p.astype(BF16), v_ref[:, col], preferred_element_type=F32)
            for p, col in zip(expo, cols)
        ]
        found = []
        for i in range(len(targets)):
            stat = jnp.zeros((tokens, HD), F32)
            for j in range(heads_dev):
                stat = jnp.where(lane == j, peaks[i * heads_dev + j], stat)
                stat = jnp.where(lane == mid + j, totals[i * heads_dev + j], stat)
            found.append((sums[i * heads_dev:(i + 1) * heads_dev], stat))
        return found

    def write(ref, found):
        sums, stat = found
        for j in range(heads_dev):
            ref[j] = sums[j].astype(BF16)
        ref[heads_dev] = stat.astype(BF16)

    def merge(found, refs):
        sums, stat = found
        stats = [stat] + [ref[heads_dev].astype(F32) for ref in refs]
        best = functools.reduce(jnp.maximum, stats)
        factors = [jnp.exp2(s - best) for s in stats]
        total = sum(s * pltpu.roll(f, mid, 1) for s, f in zip(stats, factors))
        merged = []
        for j in range(heads_dev):
            o = sums[j] * factors[0][:, j:j + 1]
            for ref, f in zip(refs, factors[1:]):
                o = o + ref[j].astype(F32) * f[:, j:j + 1]
            merged.append(o)
        return merged, jnp.where(lane < mid, best, total)

    def core_copy(slot):
        return send(sb_core.at[slot], rb_core.at[slot], core_s.at[slot], core_r.at[slot], sibling)

    def y_copy(zz):
        return send(sb_y.at[zz], rb_y.at[zz], y_s.at[zz], y_r.at[zz], across)

    def z_copy(zz, sender):
        return send(sb_z.at[zz], rb_z.at[sender], z_s.at[zz], z_r.at[sender], dev(zz, y, c))

    def for_sibling(pair, yy):
        slots = [zz * 2 + yy for zz in pair]
        for slot, found in zip(slots, attend([slot * 2 + 1 - c for slot in slots])):
            write(sb_core.at[slot], found)
            core_copy(slot).start()

    def for_across(pair):
        slots = [zz * 2 + 1 - y for zz in pair]
        both = attend([slot * 2 + c for slot in slots])
        for zz, slot, found in zip(pair, slots, both):
            core_copy(slot).wait_recv()
            write(sb_y.at[zz], merge(found, [rb_core.at[slot]]))
            y_copy(zz).start()

    def ring_pair(i):
        return [lax.rem(z + 1 + 2 * i, outer), lax.rem(z + 2 + 2 * i, outer)]

    def pairs_of(part, step):
        def body(i, carry):
            first = part * (outer // 2) + 2 * i
            step([first, first + 1])
            return carry

        lax.fori_loop(0, outer // 4, body, 0)

    pairs_of(0, lambda pair: for_sibling(pair, 1 - y))
    from_across(1)
    pairs_of(0, for_across)
    from_sibling(1)
    pairs_of(1, lambda pair: for_sibling(pair, 1 - y))
    pairs_of(1, for_across)

    def own_line(i, carry):
        for_sibling(ring_pair(i), y)
        return carry

    lax.fori_loop(0, outer // 2, own_line, 0)

    def collect(zz, found):
        slot = zz * 2 + y
        core_copy(slot).wait_recv()
        y_copy(zz).wait_recv()
        return merge(found, [rb_core.at[slot], rb_y.at[zz]])

    def for_z(i, carry):
        pair = ring_pair(i)
        for zz, found in zip(pair, attend([zz * 4 + y * 2 + c for zz in pair])):
            write(sb_z.at[zz], collect(zz, found))
            z_copy(zz, z).start()
        return carry

    lax.fori_loop(0, outer // 2 - 1, for_z, 0)
    final = zs[-2]
    found, mine = attend([final * 4 + y * 2 + c, me])
    write(sb_z.at[final], collect(final, found))
    z_copy(final, z).start()
    mine = collect(z, mine)

    section = lax.div(me * heads_dev, HEADS)

    def column(first):
        rows = jnp.zeros((n, HD), F32)
        for s in range(CONTROLS):
            found_rows = qf[pl.ds(2 * part_rows + first + s, n, stride=block_rows), :]
            rows = jnp.where(section == s, found_rows, rows)
        return jnp.concatenate([rows[:, r:r + 1] for r in range(tokens_dev)], axis=0)

    block = lax.broadcasted_iota(jnp.int32, (n, 1), 0).astype(F32)
    line = jnp.floor((block + 0.5) * (1.0 / outer))
    position = ((block - line * outer) * 4 + line) * tokens_dev
    position = jnp.concatenate([position + r for r in range(tokens_dev)], axis=0)
    is_base = section >= CONTROLS
    owner = jnp.where(is_base, position, column(0))
    level = jnp.where(is_base, float(LEVELS), column(8))
    holder = jnp.floor((owner + 0.5) * (1.0 / tokens_dev))
    chip = jnp.floor(holder * 0.5)
    z_of = jnp.floor(holder * 0.25)
    order = (holder - 2 * chip) * (n // 2) + (chip - 2 * z_of) * outer + z_of
    place = order * tokens_dev + owner - holder * tokens_dev
    picked = lax.broadcasted_iota(jnp.int32, (tokens, tokens), 1) == place.astype(jnp.int32)
    picked = picked.astype(F32).T.astype(BF16)
    level = jnp.broadcast_to(level, (tokens, HD)).astype(BF16)
    row_weight = jnp.dot(picked, level, preferred_element_type=F32)[:, 0:1] / LEVELS

    for zz in zs[:-1]:
        z_copy(zz, zz).wait_recv()
    sums, stat = merge(mine, [rb_z.at[zz] for zz in zs[:-1]])
    attended = jnp.concatenate(
        [(sums[j] / stat[:, mid + j:mid + j + 1]).astype(BF16) for j in range(heads_dev)], axis=1
    )
    chosen = jnp.dot(picked, attended, preferred_element_type=F32).astype(BF16)

    loads[5].wait()
    half, piece = tokens // 2 * SUB, tokens_dev * SUB

    def rows_at(first, count):
        return pl.ds(pl.multiple_of(first, SUB), count)

    def pc_copy(cc):
        rows = rows_at((1 - c) * half, half)
        return send(pb.at[cc, rows], rc.at[cc], pc_s.at[cc], pc_r.at[cc], sibling)

    def p_copy(zz, yy, sender_z, sender_y):
        return send(
            sp.at[yy * outer + zz], rp.at[sender_y * outer + sender_z],
            p_s.at[yy * outer + zz], p_r.at[sender_y * outer + sender_z], dev(zz, yy, c),
        )

    width = 4 * HD
    for cc in range(chunks):
        for g in range(SUB * HD // width):
            first = cc * SUB * HD + g * width
            product = jnp.dot(
                chosen, w_ref[:, first:first + width], preferred_element_type=F32
            ) * row_weight
            for t in range(width // HD):
                pf[cc, pl.ds(g * (width // HD) + t, tokens, stride=SUB), :] = (
                    product[:, t * HD:(t + 1) * HD]
                )
        rows = rows_at((1 - c) * half, half)
        pb[cc, rows] = pf[cc, rows].astype(BF16)
        pc_copy(cc).start()

    for cc in range(chunks):
        pc_copy(cc).wait_recv()

    def partial_sum(cc, zz, yy):
        at = (yy * outer + zz) * piece
        return pf[cc, rows_at(c * half + at, piece)] + rc[cc, rows_at(at, piece)].astype(F32)

    peers = [(zz, yy) for zz in zs[:-1] for yy in (1 - y, y)] + [(z, 1 - y)]
    for zz, yy in peers:
        for cc in range(chunks):
            sp[yy * outer + zz, cc] = partial_sum(cc, zz, yy).astype(BF16)
        p_copy(zz, yy, z, y).start()
    totals = [partial_sum(cc, z, y) for cc in range(chunks)]
    for zz, yy in peers:
        p_copy(zz, yy, zz, yy).wait_recv()
    for cc in range(chunks):
        total = totals[cc]
        for zz, yy in peers:
            total = total + rp[yy * outer + zz, cc].astype(F32)
        done[...] = total
        for t in range(SUB):
            out_ref[:, (cc * SUB + t) * HD:(cc * SUB + t + 1) * HD] = (
                done[pl.ds(t, tokens_dev, stride=SUB), :].astype(BF16)
            )

    for part in range(2):
        for zz in zs[:-1]:
            along(part, zz, z).wait_send()
        for zz in range(outer):
            cross(part, zz).wait_send()
        hand(part, 0).wait_send()
        hand(part, 1).wait_send()
    for slot in range(2 * outer):
        core_copy(slot).wait_send()
    for zz in range(outer):
        y_copy(zz).wait_send()
    for zz in zs[:-1]:
        z_copy(zz, z).wait_send()
    for cc in range(chunks):
        pc_copy(cc).wait_send()
    for zz, yy in peers:
        p_copy(zz, yy, z, y).wait_send()


def on_device(queries, key_rows, value_rows, out_weight, levels, owner_map):
    n = lax.axis_size("seq")
    outer = n // 4
    tokens_dev, width = queries.shape
    pairs = width // HD
    heads_dev = out_weight.shape[0] // HD
    model = out_weight.shape[1]
    tokens = tokens_dev * n
    keys = key_rows.shape[0]
    chunks = model // (SUB * HD)
    block_rows = tokens_dev * pairs + SUB

    cfg = (n, outer, tokens_dev, heads_dev, pairs, chunks)
    message = (heads_dev + 1, tokens, HD)
    vmem = pltpu.VMEM
    dma = pltpu.SemaphoreType.DMA
    return pl.pallas_call(
        functools.partial(kernel, cfg),
        out_shape=jax.ShapeDtypeStruct((tokens_dev, model), BF16),
        in_specs=[pl.BlockSpec(memory_space=pl.ANY)] * 6,
        out_specs=pl.BlockSpec(memory_space=pltpu.VMEM),
        scratch_shapes=[
            vmem(key_rows.shape, BF16),
            vmem(value_rows.shape, BF16),
            vmem(out_weight.shape, BF16),
            vmem(queries.shape, BF16),
            vmem(levels.shape, jnp.int32),
            vmem(owner_map.shape, jnp.int32),
            vmem((block_rows, HD), F32),
            vmem((n, block_rows // 2 - SUB // 2, HD), BF16),
            vmem((n, block_rows // 2 + SUB // 2, HD), BF16),
            vmem((n * block_rows, HD), F32),
            vmem((pairs, tokens, HD), BF16),
            vmem((n // 2,) + message, BF16),
            vmem((n // 2,) + message, BF16),
            vmem((outer,) + message, BF16),
            vmem((outer,) + message, BF16),
            vmem((outer,) + message, BF16),
            vmem((outer,) + message, BF16),
            vmem((chunks, tokens * SUB, HD), F32),
            vmem((chunks, tokens * SUB, HD), BF16),
            vmem((chunks, tokens // 2 * SUB, HD), BF16),
            vmem((2 * outer, chunks, tokens_dev * SUB, HD), BF16),
            vmem((2 * outer, chunks, tokens_dev * SUB, HD), BF16),
            vmem((tokens_dev * SUB, HD), F32),
            dma((6,)),
            dma((2, 2 * outer + 2)),
            dma((2, 2 * outer + 2)),
            dma((n // 2,)),
            dma((n // 2,)),
            dma((outer,)),
            dma((outer,)),
            dma((outer,)),
            dma((outer,)),
            dma((chunks,)),
            dma((chunks,)),
            dma((2 * outer,)),
            dma((2 * outer,)),
        ],
        compiler_params=pltpu.CompilerParams(
            collective_id=0, has_side_effects=True, vmem_limit_bytes=56 * 1024 * 1024
        ),
        cost_estimate=pl.CostEstimate(
            flops=4 * tokens * keys * width + 2 * tokens * heads_dev * HD * model,
            bytes_accessed=2 * (2 * keys * width + heads_dev * HD * model),
            transcendentals=tokens * keys * pairs,
        ),
    )(queries, key_rows, value_rows, out_weight, levels, owner_map)


def solution(mesh):
    return jax.shard_map(
        on_device,
        mesh=mesh,
        in_specs=(
            P(("groups", "seq"), None),
            P(("groups", "seq"), None),
            P(("groups", "seq"), None),
            P("seq", None),
            P(None, ("groups", "seq")),
            P(None, ("groups", "seq")),
        ),
        out_specs=P(("groups", "seq"), None),
        check_vma=False,
    )
```

```python
import functools
import math

import jax
import jax.numpy as jnp
from jax import lax
from jax.experimental import pallas as pl
from jax.experimental.pallas import tpu as pltpu
from jax.sharding import PartitionSpec as P

HD = 128
HEADS = 16
CONTROLS = 3
LEVELS = 8
SUB = 16
MESH = pl.DeviceIdType.MESH
F32 = jnp.float32
BF16 = jnp.bfloat16


def kernel(
    cfg, q_hbm, k_hbm, v_hbm, w_hbm, level_hbm, owner_hbm, out_ref,
    k_ref, v_ref, w_ref, q_ref, level_ref, owner_ref, qs, qg0, qg1, qf, qh,
    sb_core, rb_core, sb_y, rb_y, sb_z, rb_z,
    pf, pb, rc, sp, rp, done,
    load_sem, ag_send, ag_recv,
    core_s, core_r, y_s, y_r, z_s, z_r,
    pc_s, pc_r, p_s, p_r,
):
    n, outer, tokens_dev, heads_dev, pairs, chunks = cfg
    tokens = tokens_dev * n
    group = lax.axis_index("groups")
    me = lax.axis_index("seq")
    z, low = lax.div(me, 4), lax.rem(me, 4)
    y, c = lax.div(low, 2), lax.rem(low, 2)
    zs = [lax.rem(z + step, outer) for step in range(1, outer)] + [z]

    def dev(zz, yy, cc):
        return (group, zz * 4 + yy * 2 + cc)

    sibling, across = dev(z, y, 1 - c), dev(z, 1 - y, c)

    loads = [
        pltpu.make_async_copy(src, dst, load_sem.at[i])
        for i, (src, dst) in enumerate(
            [
                (q_hbm, q_ref), (level_hbm, level_ref), (owner_hbm, owner_ref),
                (k_hbm, k_ref), (v_hbm, v_ref), (w_hbm, w_ref),
            ]
        )
    ]
    for load in loads[:3]:
        load.start()

    barrier = pltpu.get_barrier_semaphore()
    pl.semaphore_signal(barrier, inc=1, device_id=sibling, device_id_type=MESH)
    pl.semaphore_signal(barrier, inc=1, device_id=across, device_id_type=MESH)
    for zz in zs[:-1]:
        for yy in (y, 1 - y):
            pl.semaphore_signal(
                barrier, inc=1, device_id=dev(zz, yy, c), device_id_type=MESH
            )

    def send(src, dst, s_sem, r_sem, target):
        return pltpu.make_async_remote_copy(
            src_ref=src, dst_ref=dst, send_sem=s_sem, recv_sem=r_sem,
            device_id=target, device_id_type=MESH,
        )

    part_heads = pairs // 2
    part_rows = tokens_dev * part_heads
    block_rows = 2 * part_rows + SUB
    for load in loads[:3]:
        load.wait()
    for h in range(pairs):
        first = h // part_heads * part_rows + h % part_heads
        qs[pl.ds(first, tokens_dev, stride=part_heads), :] = (
            q_ref[:, h * HD:(h + 1) * HD].astype(F32)
        )
    qs[2 * part_rows:, :] = jnp.zeros((SUB, HD), F32)
    qs[2 * part_rows:2 * part_rows + CONTROLS, 0:tokens_dev] = owner_ref[...].astype(F32)
    qs[2 * part_rows + 8:2 * part_rows + 8 + CONTROLS, 0:tokens_dev] = level_ref[...].astype(F32)
    place_of = (y * 2 + c) * outer
    mine_at = place_of + z
    qg0[mine_at] = qs[0:part_rows, :].astype(BF16)
    qg1[mine_at] = qs[part_rows:, :].astype(BF16)
    qf[pl.ds(pl.multiple_of(mine_at * block_rows, SUB), block_rows), :] = qs[...]

    pl.semaphore_wait(barrier, 2 * outer)

    parts = (qg0, qg1)
    across_at = ((1 - y) * 2 + c) * outer

    def along(part, target_z, sender_z):
        ref = parts[part].at[mine_at]
        return send(
            ref, ref, ag_send.at[part, target_z], ag_recv.at[part, sender_z], dev(target_z, y, c)
        )

    def cross(part, zz):
        ref = parts[part].at[place_of + zz]
        return send(ref, ref, ag_send.at[part, outer + zz], ag_recv.at[part, outer + zz], across)

    def hand(part, second):
        ref = parts[part].at[pl.ds(across_at if second else place_of, outer)]
        slot = 2 * outer + second
        return send(ref, ref, ag_send.at[part, slot], ag_recv.at[part, slot], sibling)

    for part in range(2):
        for zz in zs[:-1]:
            along(part, zz, z).start()
        cross(part, z).start()
    loads[3].start()
    loads[4].start()

    def widen(part, block):
        first = block * block_rows + part * part_rows
        count = part_rows + part * SUB
        qf[pl.ds(pl.multiple_of(first, SUB), count), :] = parts[part][block].astype(F32)

    def from_z(part):
        for zz in zs[:-1]:
            along(part, zz, zz).wait_recv()
            cross(part, zz).start()
        hand(part, 0).start()
        for zz in zs[:-1]:
            widen(part, place_of + zz)

    def from_across(part):
        for zz in zs[-1:] + zs[:-1]:
            cross(part, zz).wait_recv()
        hand(part, 1).start()
        for zz in zs:
            widen(part, across_at + zz)

    def from_sibling(part):
        for second, yy in ((0, y), (1, 1 - y)):
            hand(part, second).wait_recv()
            for zz in range(outer):
                widen(part, (yy * 2 + 1 - c) * outer + zz)
        for h in range(part_heads):
            qh[part * part_heads + h] = jnp.concatenate(
                [
                    qf[pl.ds(part * part_rows + r * part_heads + h, n, stride=block_rows), :]
                    for r in range(tokens_dev)
                ],
                axis=0,
            ).astype(BF16)

    from_z(0)
    from_across(0)
    from_z(1)
    loads[5].start()
    from_sibling(0)
    loads[3].wait()
    loads[4].wait()

    log_scale = HD ** -0.5 * math.log2(math.e)
    lane = lax.broadcasted_iota(jnp.int32, (tokens, HD), 1)
    mid = HD // 2

    def attend(targets):
        heads = [t * heads_dev + j for t in targets for j in range(heads_dev)]
        cols = [pl.ds(pl.multiple_of(h * HD, HD), HD) for h in heads]
        scores = [
            lax.dot_general(
                qh[h], k_ref[:, col], (((1,), (1,)), ((), ())), preferred_element_type=F32
            ) * log_scale
            for h, col in zip(heads, cols)
        ]
        peaks = [jnp.max(s, axis=1, keepdims=True).astype(BF16).astype(F32) for s in scores]
        expo = [jnp.exp2(s - m) for s, m in zip(scores, peaks)]
        totals = [jnp.sum(p, axis=1, keepdims=True) for p in expo]
        sums = [
            jnp.dot(p.astype(BF16), v_ref[:, col], preferred_element_type=F32)
            for p, col in zip(expo, cols)
        ]
        found = []
        for i in range(len(targets)):
            stat = jnp.zeros((tokens, HD), F32)
            for j in range(heads_dev):
                stat = jnp.where(lane == j, peaks[i * heads_dev + j], stat)
                stat = jnp.where(lane == mid + j, totals[i * heads_dev + j], stat)
            found.append((sums[i * heads_dev:(i + 1) * heads_dev], stat))
        return found

    def write(ref, found):
        sums, stat = found
        for j in range(heads_dev):
            ref[j] = sums[j].astype(BF16)
        ref[heads_dev] = stat.astype(BF16)

    def merge(found, refs):
        sums, stat = found
        stats = [stat] + [ref[heads_dev].astype(F32) for ref in refs]
        best = functools.reduce(jnp.maximum, stats)
        factors = [jnp.exp2(s - best) for s in stats]
        total = sum(s * pltpu.roll(f, mid, 1) for s, f in zip(stats, factors))
        merged = []
        for j in range(heads_dev):
            o = sums[j] * factors[0][:, j:j + 1]
            for ref, f in zip(refs, factors[1:]):
                o = o + ref[j].astype(F32) * f[:, j:j + 1]
            merged.append(o)
        return merged, jnp.where(lane < mid, best, total)

    def core_copy(slot):
        return send(sb_core.at[slot], rb_core.at[slot], core_s.at[slot], core_r.at[slot], sibling)

    def y_copy(zz):
        return send(sb_y.at[zz], rb_y.at[zz], y_s.at[zz], y_r.at[zz], across)

    def z_copy(zz, sender):
        return send(sb_z.at[zz], rb_z.at[sender], z_s.at[zz], z_r.at[sender], dev(zz, y, c))

    def for_sibling(pair, yy):
        slots = [zz * 2 + yy for zz in pair]
        for slot, found in zip(slots, attend([slot * 2 + 1 - c for slot in slots])):
            write(sb_core.at[slot], found)
            core_copy(slot).start()

    def for_across(pair):
        slots = [zz * 2 + 1 - y for zz in pair]
        both = attend([slot * 2 + c for slot in slots])
        for zz, slot, found in zip(pair, slots, both):
            core_copy(slot).wait_recv()
            write(sb_y.at[zz], merge(found, [rb_core.at[slot]]))
            y_copy(zz).start()

    def ring_pair(i):
        return [lax.rem(z + 1 + 2 * i, outer), lax.rem(z + 2 + 2 * i, outer)]

    def pairs_of(part, step):
        def body(i, carry):
            first = part * (outer // 2) + 2 * i
            step([first, first + 1])
            return carry

        lax.fori_loop(0, outer // 4, body, 0)

    pairs_of(0, lambda pair: for_sibling(pair, 1 - y))
    from_across(1)
    pairs_of(0, for_across)
    from_sibling(1)
    pairs_of(1, lambda pair: for_sibling(pair, 1 - y))
    pairs_of(1, for_across)

    def own_line(i, carry):
        for_sibling(ring_pair(i), y)
        return carry

    lax.fori_loop(0, outer // 2, own_line, 0)

    def collect(zz, found):
        slot = zz * 2 + y
        core_copy(slot).wait_recv()
        y_copy(zz).wait_recv()
        return merge(found, [rb_core.at[slot], rb_y.at[zz]])

    def for_z(i, carry):
        pair = ring_pair(i)
        for zz, found in zip(pair, attend([zz * 4 + y * 2 + c for zz in pair])):
            write(sb_z.at[zz], collect(zz, found))
            z_copy(zz, z).start()
        return carry

    lax.fori_loop(0, outer // 2 - 1, for_z, 0)
    final = zs[-2]
    found, mine = attend([final * 4 + y * 2 + c, me])
    write(sb_z.at[final], collect(final, found))
    z_copy(final, z).start()
    mine = collect(z, mine)

    section = lax.div(me * heads_dev, HEADS)

    def column(first):
        rows = jnp.zeros((n, HD), F32)
        for s in range(CONTROLS):
            found_rows = qf[pl.ds(2 * part_rows + first + s, n, stride=block_rows), :]
            rows = jnp.where(section == s, found_rows, rows)
        return jnp.concatenate([rows[:, r:r + 1] for r in range(tokens_dev)], axis=0)

    block = lax.broadcasted_iota(jnp.int32, (n, 1), 0).astype(F32)
    line = jnp.floor((block + 0.5) * (1.0 / outer))
    position = ((block - line * outer) * 4 + line) * tokens_dev
    position = jnp.concatenate([position + r for r in range(tokens_dev)], axis=0)
    is_base = section >= CONTROLS
    owner = jnp.where(is_base, position, column(0))
    level = jnp.where(is_base, float(LEVELS), column(8))
    holder = jnp.floor((owner + 0.5) * (1.0 / tokens_dev))
    chip = jnp.floor(holder * 0.5)
    z_of = jnp.floor(holder * 0.25)
    order = (holder - 2 * chip) * (n // 2) + (chip - 2 * z_of) * outer + z_of
    place = order * tokens_dev + owner - holder * tokens_dev
    picked = lax.broadcasted_iota(jnp.int32, (tokens, tokens), 1) == place.astype(jnp.int32)
    picked = picked.astype(F32).T.astype(BF16)
    level = jnp.broadcast_to(level, (tokens, HD)).astype(BF16)
    row_weight = jnp.dot(picked, level, preferred_element_type=F32)[:, 0:1] / LEVELS

    for zz in zs[:-1]:
        z_copy(zz, zz).wait_recv()
    sums, stat = merge(mine, [rb_z.at[zz] for zz in zs[:-1]])
    attended = jnp.concatenate(
        [(sums[j] / stat[:, mid + j:mid + j + 1]).astype(BF16) for j in range(heads_dev)], axis=1
    )
    chosen = jnp.dot(picked, attended, preferred_element_type=F32).astype(BF16)

    loads[5].wait()
    half, piece = tokens // 2 * SUB, tokens_dev * SUB

    def rows_at(first, count):
        return pl.ds(pl.multiple_of(first, SUB), count)

    def pc_copy(cc):
        rows = rows_at((1 - c) * half, half)
        return send(pb.at[cc, rows], rc.at[cc], pc_s.at[cc], pc_r.at[cc], sibling)

    def p_copy(zz, yy, sender_z, sender_y):
        return send(
            sp.at[yy * outer + zz], rp.at[sender_y * outer + sender_z],
            p_s.at[yy * outer + zz], p_r.at[sender_y * outer + sender_z], dev(zz, yy, c),
        )

    width = 4 * HD
    for cc in range(chunks):
        for g in range(SUB * HD // width):
            first = cc * SUB * HD + g * width
            product = jnp.dot(
                chosen, w_ref[:, first:first + width], preferred_element_type=F32
            ) * row_weight
            for t in range(width // HD):
                pf[cc, pl.ds(g * (width // HD) + t, tokens, stride=SUB), :] = (
                    product[:, t * HD:(t + 1) * HD]
                )
        rows = rows_at((1 - c) * half, half)
        pb[cc, rows] = pf[cc, rows].astype(BF16)
        pc_copy(cc).start()

    for cc in range(chunks):
        pc_copy(cc).wait_recv()

    def partial_sum(cc, zz, yy):
        at = (yy * outer + zz) * piece
        return pf[cc, rows_at(c * half + at, piece)] + rc[cc, rows_at(at, piece)].astype(F32)

    peers = [(zz, yy) for zz in zs[:-1] for yy in (1 - y, y)] + [(z, 1 - y)]
    for zz, yy in peers:
        for cc in range(chunks):
            sp[yy * outer + zz, cc] = partial_sum(cc, zz, yy).astype(BF16)
        p_copy(zz, yy, z, y).start()
    totals = [partial_sum(cc, z, y) for cc in range(chunks)]
    for zz, yy in peers:
        p_copy(zz, yy, zz, yy).wait_recv()
    for cc in range(chunks):
        total = totals[cc]
        for zz, yy in peers:
            total = total + rp[yy * outer + zz, cc].astype(F32)
        done[...] = total
        for t in range(SUB):
            out_ref[:, (cc * SUB + t) * HD:(cc * SUB + t + 1) * HD] = (
                done[pl.ds(t, tokens_dev, stride=SUB), :].astype(BF16)
            )

    for part in range(2):
        for zz in zs[:-1]:
            along(part, zz, z).wait_send()
        for zz in range(outer):
            cross(part, zz).wait_send()
        hand(part, 0).wait_send()
        hand(part, 1).wait_send()
    for slot in range(2 * outer):
        core_copy(slot).wait_send()
    for zz in range(outer):
        y_copy(zz).wait_send()
    for zz in zs[:-1]:
        z_copy(zz, z).wait_send()
    for cc in range(chunks):
        pc_copy(cc).wait_send()
    for zz, yy in peers:
        p_copy(zz, yy, z, y).wait_send()


def on_device(queries, key_rows, value_rows, out_weight, levels, owner_map):
    n = lax.axis_size("seq")
    outer = n // 4
    tokens_dev, width = queries.shape
    pairs = width // HD
    heads_dev = out_weight.shape[0] // HD
    model = out_weight.shape[1]
    tokens = tokens_dev * n
    keys = key_rows.shape[0]
    chunks = model // (SUB * HD)
    block_rows = tokens_dev * pairs + SUB

    cfg = (n, outer, tokens_dev, heads_dev, pairs, chunks)
    message = (heads_dev + 1, tokens, HD)
    vmem = pltpu.VMEM
    dma = pltpu.SemaphoreType.DMA
    return pl.pallas_call(
        functools.partial(kernel, cfg),
        out_shape=jax.ShapeDtypeStruct((tokens_dev, model), BF16),
        in_specs=[pl.BlockSpec(memory_space=pl.ANY)] * 6,
        out_specs=pl.BlockSpec(memory_space=pltpu.VMEM),
        scratch_shapes=[
            vmem(key_rows.shape, BF16),
            vmem(value_rows.shape, BF16),
            vmem(out_weight.shape, BF16),
            vmem(queries.shape, BF16),
            vmem(levels.shape, jnp.int32),
            vmem(owner_map.shape, jnp.int32),
            vmem((block_rows, HD), F32),
            vmem((n, block_rows // 2 - SUB // 2, HD), BF16),
            vmem((n, block_rows // 2 + SUB // 2, HD), BF16),
            vmem((n * block_rows, HD), F32),
            vmem((pairs, tokens, HD), BF16),
            vmem((n // 2,) + message, BF16),
            vmem((n // 2,) + message, BF16),
            vmem((outer,) + message, BF16),
            vmem((outer,) + message, BF16),
            vmem((outer,) + message, BF16),
            vmem((outer,) + message, BF16),
            vmem((chunks, tokens * SUB, HD), F32),
            vmem((chunks, tokens * SUB, HD), BF16),
            vmem((chunks, tokens // 2 * SUB, HD), BF16),
            vmem((2 * outer, chunks, tokens_dev * SUB, HD), BF16),
            vmem((2 * outer, chunks, tokens_dev * SUB, HD), BF16),
            vmem((tokens_dev * SUB, HD), F32),
            dma((6,)),
            dma((2, 2 * outer + 2)),
            dma((2, 2 * outer + 2)),
            dma((n // 2,)),
            dma((n // 2,)),
            dma((outer,)),
            dma((outer,)),
            dma((outer,)),
            dma((outer,)),
            dma((chunks,)),
            dma((chunks,)),
            dma((2 * outer,)),
            dma((2 * outer,)),
        ],
        compiler_params=pltpu.CompilerParams(
            collective_id=0, has_side_effects=True, vmem_limit_bytes=56 * 1024 * 1024
        ),
        cost_estimate=pl.CostEstimate(
            flops=4 * tokens * keys * width + 2 * tokens * heads_dev * HD * model,
            bytes_accessed=2 * (2 * keys * width + heads_dev * HD * model),
            transcendentals=tokens * keys * pairs,
        ),
    )(queries, key_rows, value_rows, out_weight, levels, owner_map)


def solution(mesh):
    return jax.shard_map(
        on_device,
        mesh=mesh,
        in_specs=(
            P(("groups", "seq"), None),
            P(("groups", "seq"), None),
            P(("groups", "seq"), None),
            P("seq", None),
            P(None, ("groups", "seq")),
            P(None, ("groups", "seq")),
        ),
        out_specs=P(("groups", "seq"), None),
        check_vma=False,
    )
```
